256 devices in a mesh: ctx: 32 (over x, z), tp: 8 (over y, core).
Axes of the slice: x: 4, y: 4, z: 8, core: 2. Of those that a mesh axis runs over, the one named last changes fastest.
Arguments:
- head_input: bfloat16 [16384, 4096], P('ctx', 'tp'), may hold values from -6 to 6
- write_vector: bfloat16 [16384, 128], P('ctx'), may hold values from -0.119628906 to 0.119628906
- read_vector: bfloat16 [16384, 128], P('ctx'), may hold values from -0.5 to 0.5
- log_decay: float32 [64, 16384], P('tp', 'ctx'), may hold values from -1 to 0
- skip_gain: float32 [64], P('tp'), may hold values from 0.5 to 2
- out_grad: bfloat16 [16384, 4096], P('ctx'), may hold values from -12 to 12
- out_master: float32 [4096, 4096], P('ctx', 'tp'), may hold values from -0.09375 to 0.09375
- first_moment: float32 [4096, 4096], P('ctx', 'tp'), may hold values from -180 to 180
- squared_average: float32 [64], P('tp'), may hold values from 16.384 to 163.84
Outputs:
- input_grad: bfloat16 [16384, 4096], P('ctx', 'tp')
- write_grad: float32 [16384, 128], P('ctx')
- read_grad: float32 [16384, 128], P('ctx')
- decay_grad: float32 [64, 16384], P('tp', 'ctx')
- skip_grad: float32 [64], P('tp')
- new_master: float32 [4096, 4096], P('ctx', 'tp')
- new_first: float32 [4096, 4096], P('ctx', 'tp')
- new_second: float32 [64], P('tp')
The draws below stay inside these ranges and needn't reach their ends.
All inputs are finite; a program needn't handle non-finite values.
Results may differ from the reference program's by a relative error of at most 0.008.
Values may be sent and summed in bfloat16 or wider, within the bound.
No kernel may reach another device: no remote copies, remote signals or barrier semaphores. Data moves between devices by JAX's collectives and lax.ppermute only.
A program may use at most 128 MiB of HBM per device.

```python
import math
import jax
import jax.numpy as jnp
from jax import lax

WIDTH = 4096
SHARD_HEAD_COUNT = 64
HEAD_DIM = 64
STATE = 128
TOK_DEV = 512
CONTEXT_LENGTH = 16384
INNER = 4096


def draw_log_decay(key, part):
    key = jax.random.fold_in(key, 11)
    sampler_seeds = jax.random.split(key, 6)
    share = 0.5
    fast_heads = jax.random.uniform(sampler_seeds[0], (SHARD_HEAD_COUNT, 1)) < share
    fast_rate = jnp.exp(jax.random.uniform(sampler_seeds[1], (SHARD_HEAD_COUNT, 1), minval=-0.3, maxval=0.3)) / 40.0
    slow_rate = 0.9 / CONTEXT_LENGTH
    block_scale = jnp.exp(jax.random.uniform(sampler_seeds[2], (SHARD_HEAD_COUNT, CONTEXT_LENGTH // TOK_DEV, 1), minval=-0.7, maxval=0.7))
    block_scale = jnp.broadcast_to(block_scale, (SHARD_HEAD_COUNT, CONTEXT_LENGTH // TOK_DEV, TOK_DEV)).reshape(SHARD_HEAD_COUNT, CONTEXT_LENGTH)
    token_scale = jax.random.uniform(sampler_seeds[3], (SHARD_HEAD_COUNT, CONTEXT_LENGTH), minval=0.5, maxval=1.5)
    update_factor = jnp.where(fast_heads, fast_rate, slow_rate) * block_scale * token_scale
    transfer_bundles = jax.random.uniform(sampler_seeds[4], (SHARD_HEAD_COUNT, CONTEXT_LENGTH)) < 2.0 / CONTEXT_LENGTH
    dropped_summands = jnp.log(jax.random.uniform(sampler_seeds[5], (SHARD_HEAD_COUNT, CONTEXT_LENGTH), minval=0.5, maxval=0.8))
    return (jnp.where(transfer_bundles, dropped_summands, 0.0) - update_factor).astype(jnp.float32)


def draw_out_grad(key, part):
    key = jax.random.fold_in(key, 23)
    sampler_seeds = jax.random.split(key, 3)
    row_scale = jnp.exp(jax.random.uniform(sampler_seeds[0], (CONTEXT_LENGTH, 1), minval=0.0, maxval=math.log(10.0)))
    ramp = jnp.arange(WIDTH, dtype=jnp.float32)[None, :] * (math.log(3.0) / WIDTH)
    col_scale = jnp.exp(ramp + jax.random.uniform(sampler_seeds[1], (1, WIDTH), minval=0.0, maxval=math.log(10.0)))
    base = jnp.clip(jax.random.normal(sampler_seeds[2], (CONTEXT_LENGTH, WIDTH)), -5.0, 5.0)
    return (base * row_scale * col_scale / 128.0).astype(jnp.bfloat16)


def level_of(rng, shape, shards, smallest, top_value):
    gain = 1.0
    for position, shards_of in shards:
        heights = jax.random.uniform(jax.random.fold_in(jax.random.fold_in(rng, 6), position), (shards_of,), jnp.float32, smallest / len(shards), top_value / len(shards))
        gain = gain * jnp.repeat(jnp.exp(heights), shape[position] // shards_of).reshape((-1,) + (1,) * (len(shape) - 1 - position))
    return gain


def normal_values(own_key, shape, scale, most, shards=(), kind=jnp.bfloat16):
    array = jax.random.normal(own_key, shape, jnp.float32) * scale
    if len(shards) > 0:
        array = level_of(own_key, shape, shards, -0.22, 0.18) * array
    return jnp.clip(array, min=-most, max=most).astype(kind)


def setup_inputs(seed: int = 0) -> dict:
    splits = jax.random.split(jax.random.key(seed), 10)
    return {
        "head_input": normal_values(splits[0], (CONTEXT_LENGTH, INNER), 1.0, 6.0, ((0, 32), (1, 8))),
        "write_vector": normal_values(splits[1], (CONTEXT_LENGTH, STATE), 0.02, 0.119628906, ((0, 32),)),
        "read_vector": normal_values(splits[2], (CONTEXT_LENGTH, STATE), STATE ** -0.5, 0.5, ((0, 32),)),
        "log_decay": draw_log_decay(jax.random.fold_in(splits[9], 71), 0),
        "skip_gain": jnp.clip(jnp.exp(math.log(2.0) - 1.3862944 * jax.random.uniform(splits[4], (SHARD_HEAD_COUNT,), jnp.float32) ** level_of(splits[4], (SHARD_HEAD_COUNT,), ((0, 8),), -0.2, 0.2)), 0.5, 2.0),
        "out_grad": draw_out_grad(jax.random.fold_in(splits[9], 71), 0),
        "out_master": normal_values(splits[6], (WIDTH, INNER), INNER ** -0.5, 0.09375, ((0, 32), (1, 8)), jnp.float32),
        "first_moment": normal_values(splits[7], (WIDTH, INNER), 30.0, 180.0, ((0, 32), (1, 8)), jnp.float32),
        "squared_average": jnp.clip(jnp.exp(math.log(163.84) - 2.30258502 * jax.random.uniform(splits[8], (SHARD_HEAD_COUNT,), jnp.float32) ** level_of(splits[8], (SHARD_HEAD_COUNT,), ((0, 8),), -0.2, 0.2)), 16.384, 163.84),
    }


highest = lax.Precision.HIGHEST
beta_one = 0.9
beta_two = 0.95
learn_rate = 0.004
decoupled_decay = 0.1
adam_eps = 1e-08
bias_one = 0.9999734386011124
bias_two = 0.994079470779666

def decay_tables(block_log):
    running = jnp.cumsum(block_log, axis=1)
    last_sum = running[:, -1:]
    gap = running[:, :, None] - running[:, None, :]
    row_index = lax.broadcasted_iota(jnp.int32, gap.shape, 1)
    col_index = lax.broadcasted_iota(jnp.int32, gap.shape, 2)
    lower_decay = jnp.exp(jnp.where(row_index >= col_index, gap, -1e+30))
    to_end = jnp.exp(last_sum - running)
    from_start = jnp.exp(running)
    return (lower_decay, to_end, from_start, jnp.exp(last_sum[:, 0]))

def chain_terms(head_x, write_b, read_c, output_gradient, to_end, from_start):
    local_state = jnp.einsum('shp,sn->hpn', head_x * to_end.T[:, :, None], write_b, precision=highest)
    carried = jnp.einsum('shp,sn->hpn', output_gradient * from_start.T[:, :, None], read_c, precision=highest)
    return (local_state, carried)

def finish_block(head_x, write_b, read_c, output_gradient, skip_gain, lower_decay, to_end, from_start, start_state, end_adjoint):
    scores = jnp.dot(read_c, write_b.T, precision=highest)
    blended_reduced = (lower_decay * scores[None]).astype(jnp.bfloat16)
    blended_reduced = lax.optimization_barrier(blended_reduced)
    mixed = blended_reduced.astype(jnp.float32)
    core_y = jnp.einsum('hts,shp->thp', mixed, head_x, precision=highest)
    core_y = core_y + jnp.einsum('hpn,tn->thp', start_state, read_c, precision=highest) * from_start.T[:, :, None]
    out_y = (core_y + skip_gain[None, :, None] * head_x).astype(jnp.bfloat16)
    core_grad = jnp.einsum('hst,shp->thp', mixed, output_gradient, precision=highest)
    core_grad = core_grad + jnp.einsum('hpn,tn->thp', end_adjoint, write_b, precision=highest) * to_end.T[:, :, None]
    input_grad = (core_grad + skip_gain[None, :, None] * output_gradient).astype(jnp.bfloat16)
    cross_dots = jnp.einsum('thp,shp->hts', output_gradient, head_x, precision=highest)
    pair_weights = lax.optimization_barrier(jnp.sum(lower_decay * cross_dots, axis=0))
    read_grad = jnp.dot(pair_weights, write_b, precision=highest)
    read_grad = read_grad + jnp.einsum('hpn,thp,ht->tn', start_state, output_gradient, from_start, precision=highest)
    write_grad = lax.dot_general(pair_weights, read_c, (((0,), (0,)), ((), ())), precision=highest)
    write_grad = write_grad + jnp.einsum('hpn,thp,ht->tn', end_adjoint, head_x, to_end, precision=highest)
    skip_part = lax.optimization_barrier(jnp.sum(output_gradient * head_x, axis=(0, 2)))
    decay_part = (lax.optimization_barrier(jnp.sum(output_gradient * core_y, axis=2)) - lax.optimization_barrier(jnp.sum(head_x * core_grad, axis=2))).T
    return (out_y, input_grad, write_grad, read_grad, skip_part, decay_part)

def adam_mini(master, first, second, grad, mean_square, head_width):
    new_second = beta_two * second + (1.0 - beta_two) * mean_square
    new_first = beta_one * first + (1.0 - beta_one) * grad
    scale = jnp.repeat(jnp.sqrt(new_second / bias_two) + adam_eps, head_width)
    new_master = master - learn_rate * (new_first / bias_one / scale[None, :] + decoupled_decay * master)
    return (new_first, new_second, new_master)

def reference(head_input, write_vector, read_vector, log_decay, skip_gain, out_grad, out_master, first_moment, squared_average):
    blocks = CONTEXT_LENGTH // TOK_DEV
    weight_bf = out_master.astype(jnp.bfloat16)
    grad_flat = jnp.dot(out_grad, weight_bf, preferred_element_type=jnp.float32).astype(jnp.bfloat16)
    head_x = head_input.astype(jnp.float32).reshape(blocks, TOK_DEV, SHARD_HEAD_COUNT, HEAD_DIM)
    output_gradient = grad_flat.astype(jnp.float32).reshape(blocks, TOK_DEV, SHARD_HEAD_COUNT, HEAD_DIM)
    write_b = write_vector.astype(jnp.float32).reshape(blocks, TOK_DEV, STATE)
    read_c = read_vector.astype(jnp.float32).reshape(blocks, TOK_DEV, STATE)
    decay_blocks = log_decay.reshape(SHARD_HEAD_COUNT, blocks, TOK_DEV).transpose(1, 0, 2)

    def block_chain(inputs):
        block_x, block_b, block_c, block_dy, block_log = inputs
        lower_decay, to_end, from_start, decay_per_block = decay_tables(block_log)
        local_state, carried = chain_terms(block_x, block_b, block_c, block_dy, to_end, from_start)
        return (local_state, carried, decay_per_block)
    local_states, carried_all, block_decays = lax.map(block_chain, (head_x, write_b, read_c, output_gradient, decay_blocks))

    def forward_step(state, inputs):
        local_state, decay_per_block = inputs
        return (decay_per_block[:, None, None] * state + local_state, state)

    def backward_step(adjoint, inputs):
        carried, decay_per_block = inputs
        return (carried + decay_per_block[:, None, None] * adjoint, adjoint)
    zero_state = jnp.zeros((SHARD_HEAD_COUNT, HEAD_DIM, STATE), jnp.float32)
    final_state, start_states = lax.scan(forward_step, zero_state, (local_states, block_decays))
    first_adjoint, end_adjoints = lax.scan(backward_step, zero_state, (carried_all, block_decays), reverse=True)

    def block_finish(inputs):
        block_x, block_b, block_c, block_dy, block_log, start_state, end_adjoint = inputs
        lower_decay, to_end, from_start, decay_per_block = decay_tables(block_log)
        return finish_block(block_x, block_b, block_c, block_dy, skip_gain, lower_decay, to_end, from_start, start_state, end_adjoint)
    out_y, input_grad, write_grad, read_grad, skip_parts, decay_parts = lax.map(block_finish, (head_x, write_b, read_c, output_gradient, decay_blocks, start_states, end_adjoints))
    out_flat = out_y.reshape(CONTEXT_LENGTH, INNER)
    weight_grad = lax.dot_general(out_grad, out_flat, (((0,), (0,)), ((), ())), preferred_element_type=jnp.float32)
    decay_flat = decay_parts.transpose(1, 0, 2).reshape(SHARD_HEAD_COUNT, CONTEXT_LENGTH)
    decay_grad = jnp.flip(jnp.cumsum(jnp.flip(decay_flat, 1), axis=1), 1)
    skip_grad = lax.optimization_barrier(jnp.sum(skip_parts, axis=0))
    squares = (weight_grad * weight_grad).reshape(WIDTH, SHARD_HEAD_COUNT, HEAD_DIM)
    mean_square = lax.optimization_barrier(jnp.sum(squares, axis=(0, 2))) / float(WIDTH * HEAD_DIM)
    new_first, new_second, new_master = adam_mini(out_master, first_moment, squared_average, weight_grad, mean_square, HEAD_DIM)
    return (input_grad.reshape(CONTEXT_LENGTH, INNER), write_grad.reshape(CONTEXT_LENGTH, STATE), read_grad.reshape(CONTEXT_LENGTH, STATE), decay_grad, skip_grad, new_master, new_first, new_second)
```

```python
import jax
import jax.numpy as jnp
from jax import lax
from jax.sharding import Mesh, PartitionSpec as P

WIDTH = 4096
beta_one = 0.9
beta_two = 0.95
learn_rate = 0.004
decoupled_decay = 0.1
adam_eps = 1e-08
bias_one = 0.9999734386011124
bias_two = 0.994079470779666

f32 = jnp.float32
bf16 = jnp.bfloat16
CTX = ("x", "z")
TP = ("y", "core")
BLOCKS = 32


def mm(a, b, dims):
    return lax.dot_general(a, b, (dims, ((), ())), preferred_element_type=f32)


def block_weights(logs):
    i = lax.broadcasted_iota(jnp.int32, (BLOCKS, BLOCKS, BLOCKS), 0)
    j = lax.broadcasted_iota(jnp.int32, (BLOCKS, BLOCKS, BLOCKS), 1)
    r = lax.broadcasted_iota(jnp.int32, (BLOCKS, BLOCKS, BLOCKS), 2)
    between = jnp.sum(jnp.where((r > j) & (r < i), logs[None, None, :], 0.0), axis=2)
    rows = lax.broadcasted_iota(jnp.int32, (BLOCKS, BLOCKS), 0)
    cols = lax.broadcasted_iota(jnp.int32, (BLOCKS, BLOCKS), 1)
    return jnp.where(rows > cols, jnp.exp(between), 0.0)


def swap(value, axes):
    return lax.all_to_all(value, axes, 0, 0, tiled=True)


def chain(weights, parts, reverse):
    dims = ((0,), (0,)) if reverse else ((1,), (0,))
    flat = parts.astype(f32).reshape(BLOCKS, 16 * 128)
    out = lax.dot_general(
        weights, flat, (dims, ((), ())), precision=lax.Precision.HIGHEST, preferred_element_type=f32
    )
    return out.astype(bf16).reshape(BLOCKS, 16, 128)


def shards(
    head_input,
    write_vector,
    read_vector,
    log_decay,
    skip_gain,
    out_grad,
    out_master,
    first_moment,
    squared_average,
):
    tokens, width = head_input.shape
    heads = log_decay.shape[0]
    head_width = width // heads

    weight_all = lax.all_gather(out_master.astype(bf16), CTX, axis=0, tiled=True)

    running = jnp.cumsum(log_decay, axis=1)
    last_sum = running[:, -1:]
    gap = running[:, :, None] - running[:, None, :]
    row_index = lax.broadcasted_iota(jnp.int32, gap.shape, 1)
    col_index = lax.broadcasted_iota(jnp.int32, gap.shape, 2)
    lower_decay = jnp.exp(jnp.where(row_index >= col_index, gap, -1e30))
    to_end = jnp.exp(last_sum - running)
    from_start = jnp.exp(running)
    to_end_wide = jnp.repeat(to_end.T, head_width, axis=1)
    from_start_wide = jnp.repeat(from_start.T, head_width, axis=1)
    skip_wide = jnp.repeat(skip_gain, head_width)[None, :]

    head_x = head_input.astype(f32)
    local_state = mm((head_x * to_end_wide).astype(bf16), write_vector, ((0,), (0,)))
    total = last_sum[:, 0]
    high = lax.reduce_precision(total, 8, 7)
    middle = lax.reduce_precision(total - high, 8, 7)
    low = lax.reduce_precision(total - high - middle, 8, 7)
    pieces = jnp.stack([high, middle, low] + [jnp.zeros_like(low)] * 5, axis=1).astype(bf16)
    pieces = jnp.broadcast_to(pieces[:, None, :, None], (heads, BLOCKS // heads, 8, 128))
    packed = jnp.concatenate(
        [local_state.astype(bf16).reshape(BLOCKS, 16, 128), pieces.reshape(BLOCKS, 8, 128)], axis=1
    )
    packed = swap(packed, CTX)
    logs = jnp.sum(packed[:, 16:19, 0].astype(f32), axis=1)
    weights = block_weights(logs)
    start_low = swap(chain(weights, packed[:, :16], False), CTX).reshape(width, 128)

    scores = mm(read_vector, write_vector, ((1,), (1,)))
    mixed = (lower_decay * scores[None]).astype(bf16)
    x_heads = head_input.reshape(tokens, heads, head_width)
    inner = jnp.einsum("hts,shp->thp", mixed, x_heads, preferred_element_type=f32)
    core_y = inner.reshape(tokens, width) + mm(read_vector, start_low, ((1,), (1,))) * from_start_wide
    out_y = (core_y + skip_wide * head_x).astype(bf16)

    partial = mm(out_grad, out_y, ((0,), (0,))).astype(bf16)
    quarter = WIDTH // 4
    partial = swap(partial, "x").reshape(4, quarter, width)
    partial = jnp.sum(partial.astype(f32), axis=0).astype(bf16)
    partial = swap(partial, "z").reshape(8, quarter // 8, width)
    weight_grad = jnp.sum(partial.astype(f32), axis=0)

    grad_low = mm(out_grad, weight_all, ((1,), (0,))).astype(bf16)
    grad = grad_low.astype(f32)
    grad_decayed = (grad * from_start_wide).astype(bf16)
    carried = mm(grad_decayed, read_vector, ((0,), (0,)))
    carried = swap(carried.astype(bf16).reshape(BLOCKS, 16, 128), CTX)
    end_low = swap(chain(weights, carried, True), CTX).reshape(width, 128)

    grad_heads = grad_low.reshape(tokens, heads, head_width)
    inner = jnp.einsum("hst,shp->thp", mixed, grad_heads, preferred_element_type=f32)
    core_grad = inner.reshape(tokens, width) + mm(write_vector, end_low, ((1,), (1,))) * to_end_wide
    input_grad = (core_grad + skip_wide * grad).astype(bf16)
    cross_dots = jnp.einsum("thp,shp->hts", grad_heads, x_heads, preferred_element_type=f32)
    pair_weights = jnp.sum(lower_decay * cross_dots, axis=0).astype(bf16)
    read_grad = mm(pair_weights, write_vector, ((1,), (0,))) + mm(grad_decayed, start_low, ((1,), (0,)))
    write_grad = mm(pair_weights, read_vector, ((0,), (0,))) + mm(
        (head_x * to_end_wide).astype(bf16), end_low, ((1,), (0,))
    )
    both = jnp.concatenate([write_grad, read_grad], axis=0).astype(bf16).reshape(8, -1, 128)
    both = swap(both, TP)
    both = jnp.sum(both.astype(f32), axis=0).astype(bf16)
    both = swap(jnp.broadcast_to(both[None], (8,) + both.shape), TP)
    both = both.reshape(2 * tokens, 128).astype(f32)

    terms = (grad * core_y - head_x * core_grad).reshape(tokens, heads, head_width)
    decay_part = jnp.sum(terms, axis=2).T
    local_tail = jnp.flip(jnp.cumsum(jnp.flip(decay_part, 1), axis=1), 1)
    end_state = start_low.astype(f32).reshape(heads, -1) * jnp.exp(last_sum) + local_state.reshape(
        heads, -1
    )
    above = jnp.sum(end_state * end_low.astype(f32).reshape(heads, -1), axis=1)
    decay_grad = local_tail + above[:, None]

    skip_part = jnp.sum((grad * head_x).reshape(tokens, heads, head_width), axis=(0, 2))
    square_part = jnp.sum((weight_grad * weight_grad).reshape(-1, heads, head_width), axis=(0, 2))
    small = jnp.concatenate([skip_part, square_part])
    small = lax.psum(lax.psum(small, "x"), "z")
    skip_total, square_total = small[:heads], small[heads:]
    mean_square = square_total / float(WIDTH * head_width)
    new_second = beta_two * squared_average + (1.0 - beta_two) * mean_square
    new_first = beta_one * first_moment + (1.0 - beta_one) * weight_grad
    scale = jnp.repeat(jnp.sqrt(new_second / bias_two) + adam_eps, head_width)
    new_master = out_master - learn_rate * (
        new_first / bias_one / scale[None, :] + decoupled_decay * out_master
    )
    return (
        input_grad,
        both[:tokens],
        both[tokens:],
        decay_grad,
        skip_total,
        new_master,
        new_first,
        new_second,
    )


def solution(mesh):
    fine = Mesh(mesh.devices.reshape(4, 8, 4, 2), ("x", "z", "y", "core"))
    in_specs = (
        P(CTX, TP),
        P(CTX, None),
        P(CTX, None),
        P(TP, CTX),
        P(TP),
        P(CTX, None),
        P(CTX, TP),
        P(CTX, TP),
        P(TP),
    )
    out_specs = (
        P(CTX, TP),
        P(CTX, None),
        P(CTX, None),
        P(TP, CTX),
        P(TP),
        P(CTX, TP),
        P(CTX, TP),
        P(TP),
    )
    return jax.shard_map(shards, mesh=fine, in_specs=in_specs, out_specs=out_specs, check_vma=False)
```

```python
import jax
import jax.numpy as jnp
from jax import lax
from jax.sharding import Mesh, PartitionSpec as P

WIDTH = 4096
beta_one = 0.9
beta_two = 0.95
learn_rate = 0.004
decoupled_decay = 0.1
adam_eps = 1e-08
bias_one = 0.9999734386011124
bias_two = 0.994079470779666

f32 = jnp.float32
bf16 = jnp.bfloat16
CTX = ("x", "z")
TP = ("y", "core")
BLOCKS = 32


def mm(a, b, dims):
    return lax.dot_general(a, b, (dims, ((), ())), preferred_element_type=f32)


def block_weights(logs):
    i = lax.broadcasted_iota(jnp.int32, (BLOCKS, BLOCKS, BLOCKS), 0)
    j = lax.broadcasted_iota(jnp.int32, (BLOCKS, BLOCKS, BLOCKS), 1)
    r = lax.broadcasted_iota(jnp.int32, (BLOCKS, BLOCKS, BLOCKS), 2)
    between = jnp.sum(jnp.where((r > j) & (r < i), logs[None, None, :], 0.0), axis=2)
    rows = lax.broadcasted_iota(jnp.int32, (BLOCKS, BLOCKS), 0)
    cols = lax.broadcasted_iota(jnp.int32, (BLOCKS, BLOCKS), 1)
    return jnp.where(rows > cols, jnp.exp(between), 0.0)


def exact(a, b, dims):
    return lax.dot_general(
        a.astype(f32),
        b.astype(f32),
        (dims, ((), ())),
        precision=lax.Precision.HIGHEST,
        preferred_element_type=f32,
    )


def swap(value, axes):
    return lax.all_to_all(value, axes, 0, 0, tiled=True)


def swap_core(value):
    return lax.ppermute(value, "core", [(0, 1), (1, 0)])


def spread(value, axis, count):
    return swap(jnp.broadcast_to(value[None], (count,) + value.shape), axis)


def chain(weights, parts, reverse):
    dims = ((0,), (0,)) if reverse else ((1,), (0,))
    out = exact(weights, parts.reshape(BLOCKS, 16 * 128), dims)
    return out.reshape(BLOCKS, 16, 128)


def shards(
    head_input,
    write_vector,
    read_vector,
    log_decay,
    skip_gain,
    out_grad,
    out_master,
    first_moment,
    squared_average,
):
    tokens, width = head_input.shape
    heads = log_decay.shape[0]
    head_width = width // heads

    core = lax.axis_index("core")
    ring = lax.axis_index("x")
    half = tokens // 2
    quarter = WIDTH // 4

    weight_rows = lax.all_gather(out_master.astype(bf16), "z", axis=0, tiled=True)
    pieces_out = []
    for step in (2, 1, 3, 0):
        to = lax.rem(ring + step, 4)
        piece = lax.dynamic_slice(out_grad, (core * half, to * quarter), (half, quarter))
        if step:
            piece = lax.ppermute(piece, "x", [(i, (i + step) % 4) for i in range(4)])
        pieces_out.append(piece)

    running = jnp.cumsum(log_decay, axis=1)
    last_sum = running[:, -1:]
    gap = running[:, :, None] - running[:, None, :]
    row_index = lax.broadcasted_iota(jnp.int32, gap.shape, 1)
    col_index = lax.broadcasted_iota(jnp.int32, gap.shape, 2)
    lower_decay = jnp.exp(jnp.where(row_index >= col_index, gap, -1e30))
    to_end = jnp.exp(last_sum - running)
    from_start = jnp.exp(running)
    to_end_wide = jnp.repeat(to_end.T, head_width, axis=1)
    from_start_wide = jnp.repeat(from_start.T, head_width, axis=1)
    skip_wide = jnp.repeat(skip_gain, head_width)[None, :]

    head_x = head_input.astype(f32)
    x_decayed = head_x * to_end_wide
    local_state = exact(x_decayed, write_vector, ((0,), (0,)))
    totals = jnp.broadcast_to(last_sum[:, None, :, None], (heads, BLOCKS // heads, 8, 128))
    packed = jnp.concatenate(
        [local_state.reshape(BLOCKS, 16, 128), totals.reshape(BLOCKS, 8, 128)], axis=1
    )
    packed = swap(packed, CTX)
    pieces_out, _ = lax.optimization_barrier((pieces_out, packed))
    ring_grad = jnp.zeros((4, tokens, quarter), bf16)
    for step, piece in zip((2, 1, 3, 0), pieces_out):
        came = lax.rem(ring + 4 - step, 4)
        ring_grad = lax.dynamic_update_slice(ring_grad, piece[None], (came, core * half, 0))
        ring_grad = lax.dynamic_update_slice(
            ring_grad, swap_core(piece)[None], (came, (1 - core) * half, 0)
        )
    ring_grad = ring_grad.reshape(4 * tokens, quarter)
    weights = block_weights(packed[:, 16, 0])
    start = swap(chain(weights, packed[:, :16], False), CTX).reshape(width, 128)

    scores = mm(read_vector, write_vector, ((1,), (1,)))
    mixed = (lower_decay * scores[None]).astype(bf16)
    x_heads = head_input.reshape(tokens, heads, head_width)
    inner = jnp.einsum("hts,shp->thp", mixed, x_heads, preferred_element_type=f32)
    core_y = inner.reshape(tokens, width) + exact(read_vector, start, ((1,), (1,))) * from_start_wide
    out_y = (core_y + skip_wide * head_x).astype(bf16)

    parts = mm(ring_grad, weight_rows, ((1,), (0,))).astype(bf16).reshape(4, tokens, width)
    parts, _ = lax.optimization_barrier((parts, start))
    grad_low = jnp.sum(swap(parts, "x").astype(f32), axis=0).astype(bf16)

    ring_y = lax.all_gather(out_y, "x", axis=0, tiled=True)
    partial = mm(ring_grad, ring_y, ((0,), (0,))).astype(bf16)
    weight_grad = lax.psum_scatter(partial, "z", scatter_dimension=0, tiled=True).astype(f32)

    grad = grad_low.astype(f32)
    grad_decayed = grad * from_start_wide
    carried = exact(grad_decayed, read_vector, ((0,), (0,)))
    carried = swap(carried.reshape(BLOCKS, 16, 128), CTX)
    end = swap(chain(weights, carried, True), CTX).reshape(width, 128)

    grad_heads = grad_low.reshape(tokens, heads, head_width)
    inner = jnp.einsum("hst,shp->thp", mixed, grad_heads, preferred_element_type=f32)
    core_grad = inner.reshape(tokens, width) + exact(write_vector, end, ((1,), (1,))) * to_end_wide
    input_grad = (core_grad + skip_wide * grad).astype(bf16)
    cross_dots = jnp.einsum("thp,shp->hts", grad_heads, x_heads, preferred_element_type=f32)
    pair_weights = jnp.sum(lower_decay * cross_dots, axis=0).astype(bf16)
    read_grad = mm(pair_weights, write_vector, ((1,), (0,))) + mm(
        grad_decayed.astype(bf16), start.astype(bf16), ((1,), (0,))
    )
    write_grad = mm(pair_weights, read_vector, ((0,), (0,))) + mm(
        x_decayed.astype(bf16), end.astype(bf16), ((1,), (0,))
    )
    both = jnp.concatenate([write_grad, read_grad], axis=0)
    keep = lax.dynamic_slice_in_dim(both, core * tokens, tokens, axis=0)
    give = lax.dynamic_slice_in_dim(both, (1 - core) * tokens, tokens, axis=0)
    keep = keep + swap_core(give)
    keep = jnp.sum(spread(keep.astype(bf16), "y", 4).astype(f32), axis=0)
    give = swap_core(keep)
    write_sum = jnp.where(core == 0, keep, give)
    read_sum = jnp.where(core == 0, give, keep)

    terms = (grad * core_y - head_x * core_grad).reshape(tokens, heads, head_width)
    decay_part = jnp.sum(terms, axis=2).T
    local_tail = jnp.flip(jnp.cumsum(jnp.flip(decay_part, 1), axis=1), 1)
    end_state = start.reshape(heads, -1) * jnp.exp(last_sum) + local_state.reshape(
        heads, -1
    )
    above = jnp.sum(end_state * end.reshape(heads, -1), axis=1)
    decay_grad = local_tail + above[:, None]

    skip_part = jnp.sum((grad * head_x).reshape(tokens, heads, head_width), axis=(0, 2))
    square_part = jnp.sum((weight_grad * weight_grad).reshape(-1, heads, head_width), axis=(0, 2))
    small = jnp.concatenate([skip_part, square_part, jnp.zeros((112,), f32)])
    small = spread(jnp.broadcast_to(small[None], (8, 128)), CTX, BLOCKS)
    small = jnp.sum(small, axis=0)[0]
    skip_total, square_total = small[:heads], small[heads : 2 * heads]
    mean_square = square_total / float(WIDTH * head_width)
    new_second = beta_two * squared_average + (1.0 - beta_two) * mean_square
    new_first = beta_one * first_moment + (1.0 - beta_one) * weight_grad
    scale = jnp.repeat(jnp.sqrt(new_second / bias_two) + adam_eps, head_width)
    new_master = out_master - learn_rate * (
        new_first / bias_one / scale[None, :] + decoupled_decay * out_master
    )
    return (
        input_grad,
        write_sum,
        read_sum,
        decay_grad,
        skip_total,
        new_master,
        new_first,
        new_second,
    )


def solution(mesh):
    fine = Mesh(mesh.devices.reshape(4, 8, 4, 2), ("x", "z", "y", "core"))
    in_specs = (
        P(CTX, TP),
        P(CTX, None),
        P(CTX, None),
        P(TP, CTX),
        P(TP),
        P(CTX, None),
        P(CTX, TP),
        P(CTX, TP),
        P(TP),
    )
    out_specs = (
        P(CTX, TP),
        P(CTX, None),
        P(CTX, None),
        P(TP, CTX),
        P(TP),
        P(CTX, TP),
        P(CTX, TP),
        P(TP),
    )
    return jax.shard_map(shards, mesh=fine, in_specs=in_specs, out_specs=out_specs, check_vma=False)
```

```python
import jax
import jax.numpy as jnp
from jax import lax
from jax.experimental import pallas as pl
from jax.experimental.pallas import tpu as pltpu
from jax.sharding import Mesh, PartitionSpec as P

WIDTH = 4096
beta_one = 0.9
beta_two = 0.95
learn_rate = 0.004
decoupled_decay = 0.1
adam_eps = 1e-08
bias_one = 0.9999734386011124
bias_two = 0.994079470779666

f32 = jnp.float32
bf16 = jnp.bfloat16
CTX = ("x", "z")
TP = ("y", "core")
BLOCKS = 32


def mm(a, b, dims):
    return lax.dot_general(a, b, (dims, ((), ())), preferred_element_type=f32)


def block_weights(logs):
    i = lax.broadcasted_iota(jnp.int32, (BLOCKS, BLOCKS, BLOCKS), 0)
    j = lax.broadcasted_iota(jnp.int32, (BLOCKS, BLOCKS, BLOCKS), 1)
    r = lax.broadcasted_iota(jnp.int32, (BLOCKS, BLOCKS, BLOCKS), 2)
    between = jnp.sum(jnp.where((r > j) & (r < i), logs[None, None, :], 0.0), axis=2)
    rows = lax.broadcasted_iota(jnp.int32, (BLOCKS, BLOCKS), 0)
    cols = lax.broadcasted_iota(jnp.int32, (BLOCKS, BLOCKS), 1)
    return jnp.where(rows > cols, jnp.exp(between), 0.0)


def exact(a, b, dims):
    return lax.dot_general(
        a.astype(f32),
        b.astype(f32),
        (dims, ((), ())),
        precision=lax.Precision.HIGHEST,
        preferred_element_type=f32,
    )


def swap(value, axes):
    return lax.all_to_all(value, axes, 0, 0, tiled=True)


def swap_core(value):
    return lax.ppermute(value, "core", [(0, 1), (1, 0)])


def ring_shift(value, step):
    return lax.ppermute(value, "x", [(i, (i + step) % 4) for i in range(4)]) if step else value


def spread(value, axis, count):
    return swap(jnp.broadcast_to(value[None], (count,) + value.shape), axis)


def ring_grad_kernel(core_ref, own_ref, other_ref, weight_ref, out_ref):
    half = own_ref.shape[0]
    core = core_ref[0]
    for ref, at in ((own_ref, core), (other_ref, 1 - core)):
        out_ref[pl.ds(pl.multiple_of(at * half, half), half), :] = jnp.dot(
            ref[...], weight_ref[...], preferred_element_type=f32
        ).astype(bf16)


def ring_grad_part(core, own, other, weight_rows):
    half, quarter = own.shape
    width = weight_rows.shape[1]
    return pl.pallas_call(
        ring_grad_kernel,
        out_shape=jax.ShapeDtypeStruct((2 * half, width), bf16),
        grid=(2,),
        in_specs=[
            pl.BlockSpec(memory_space=pltpu.SMEM),
            pl.BlockSpec((half, quarter), lambda j: (0, 0)),
            pl.BlockSpec((half, quarter), lambda j: (0, 0)),
            pl.BlockSpec((quarter, width // 2), lambda j: (0, j)),
        ],
        out_specs=pl.BlockSpec((2 * half, width // 2), lambda j: (0, j)),
        cost_estimate=pl.CostEstimate(
            flops=4 * half * quarter * width, bytes_accessed=3 << 20, transcendentals=0
        ),
        compiler_params=pltpu.CompilerParams(vmem_limit_bytes=24 << 20),
        name="ring_grad",
    )(core, own, other, weight_rows)


def weight_grad_kernel(core_ref, *refs):
    owns, others, ys, out_ref = refs[:4], refs[4:8], refs[8:12], refs[12]
    half = owns[0].shape[0]
    core = core_ref[0]
    total = None
    for own, other, y in zip(owns, others, ys):
        for ref, at in ((own, core), (other, 1 - core)):
            part = lax.dot_general(
                ref[...],
                y[pl.ds(pl.multiple_of(at * half, half), half), :],
                (((0,), (0,)), ((), ())),
                preferred_element_type=f32,
            )
            total = part if total is None else total + part
    out_ref[...] = total.astype(bf16)


def weight_grad_part(core, owns, others, ys):
    half, quarter = owns[0].shape
    width = ys[0].shape[1]
    tile = 256
    return pl.pallas_call(
        weight_grad_kernel,
        out_shape=jax.ShapeDtypeStruct((quarter, width), bf16),
        grid=(quarter // tile,),
        in_specs=[pl.BlockSpec(memory_space=pltpu.SMEM)]
        + [pl.BlockSpec((half, tile), lambda j: (0, j))] * 8
        + [pl.BlockSpec((2 * half, width), lambda j: (0, 0))] * 4,
        out_specs=pl.BlockSpec((tile, width), lambda j: (j, 0)),
        cost_estimate=pl.CostEstimate(
            flops=16 * half * quarter * width, bytes_accessed=8 << 20, transcendentals=0
        ),
        compiler_params=pltpu.CompilerParams(vmem_limit_bytes=24 << 20),
        name="weight_grad",
    )(core, *owns, *others, *ys)


def chain(weights, parts, reverse):
    dims = ((0,), (0,)) if reverse else ((1,), (0,))
    out = exact(weights, parts.reshape(BLOCKS, 16 * 128), dims)
    return out.reshape(BLOCKS, 16, 128)


def shards(
    head_input,
    write_vector,
    read_vector,
    log_decay,
    skip_gain,
    out_grad,
    out_master,
    first_moment,
    squared_average,
):
    tokens, width = head_input.shape
    heads = log_decay.shape[0]
    head_width = width // heads

    core = lax.axis_index("core")
    ring = lax.axis_index("x")
    half = tokens // 2
    quarter = WIDTH // 4

    weight_rows = lax.all_gather(out_master.astype(bf16), "z", axis=0, tiled=True)
    owns = []
    for step in range(4):
        to = lax.rem(ring + step, 4)
        piece = lax.dynamic_slice(out_grad, (core * half, to * quarter), (half, quarter))
        owns.append(ring_shift(piece, step))

    running = jnp.cumsum(log_decay, axis=1)
    last_sum = running[:, -1:]
    gap = running[:, :, None] - running[:, None, :]
    row_index = lax.broadcasted_iota(jnp.int32, gap.shape, 1)
    col_index = lax.broadcasted_iota(jnp.int32, gap.shape, 2)
    lower_decay = jnp.exp(jnp.where(row_index >= col_index, gap, -1e30))
    to_end = jnp.exp(last_sum - running)
    from_start = jnp.exp(running)
    to_end_wide = jnp.repeat(to_end.T, head_width, axis=1)
    from_start_wide = jnp.repeat(from_start.T, head_width, axis=1)
    skip_wide = jnp.repeat(skip_gain, head_width)[None, :]

    head_x = head_input.astype(f32)
    x_decayed = head_x * to_end_wide
    local_state = exact(x_decayed, write_vector, ((0,), (0,)))
    totals = jnp.broadcast_to(last_sum[:, None, :, None], (heads, BLOCKS // heads, 8, 128))
    packed = jnp.concatenate(
        [local_state.reshape(BLOCKS, 16, 128), totals.reshape(BLOCKS, 8, 128)], axis=1
    )
    packed = swap(packed, CTX)
    weights = block_weights(packed[:, 16, 0])
    start = swap(chain(weights, packed[:, :16], False), CTX).reshape(width, 128)

    scores = mm(read_vector, write_vector, ((1,), (1,)))
    mixed = (lower_decay * scores[None]).astype(bf16)
    x_heads = head_input.reshape(tokens, heads, head_width)
    inner = jnp.einsum("hts,shp->thp", mixed, x_heads, preferred_element_type=f32)
    core_y = inner.reshape(tokens, width) + exact(read_vector, start, ((1,), (1,))) * from_start_wide
    out_y = (core_y + skip_wide * head_x).astype(bf16)

    owns, _ = lax.optimization_barrier((owns, start))
    others = [swap_core(piece) for piece in owns]
    core_one = jnp.full((1,), core, jnp.int32)
    parts = [
        ring_shift(ring_grad_part(core_one, owns[step], others[step], weight_rows), 4 - step)
        for step in (2, 1, 3)
    ]
    parts.append(ring_grad_part(core_one, owns[0], others[0], weight_rows))
    ring_y = [ring_shift(out_y, step) for step in range(4)]
    parts, _ = lax.optimization_barrier((parts, out_y))
    grad_low = sum(part.astype(f32) for part in parts).astype(bf16)

    partial = weight_grad_part(core_one, owns, others, ring_y)
    weight_grad = lax.psum_scatter(partial, "z", scatter_dimension=0, tiled=True).astype(f32)

    grad = grad_low.astype(f32)
    grad_decayed = grad * from_start_wide
    carried = exact(grad_decayed, read_vector, ((0,), (0,)))
    carried = swap(carried.reshape(BLOCKS, 16, 128), CTX)
    end = swap(chain(weights, carried, True), CTX).reshape(width, 128)

    grad_heads = grad_low.reshape(tokens, heads, head_width)
    inner = jnp.einsum("hst,shp->thp", mixed, grad_heads, preferred_element_type=f32)
    core_grad = inner.reshape(tokens, width) + exact(write_vector, end, ((1,), (1,))) * to_end_wide
    input_grad = (core_grad + skip_wide * grad).astype(bf16)
    cross_dots = jnp.einsum("thp,shp->hts", grad_heads, x_heads, preferred_element_type=f32)
    pair_weights = jnp.sum(lower_decay * cross_dots, axis=0).astype(bf16)
    read_grad = mm(pair_weights, write_vector, ((1,), (0,))) + mm(
        grad_decayed.astype(bf16), start.astype(bf16), ((1,), (0,))
    )
    write_grad = mm(pair_weights, read_vector, ((0,), (0,))) + mm(
        x_decayed.astype(bf16), end.astype(bf16), ((1,), (0,))
    )
    both = jnp.concatenate([write_grad, read_grad], axis=0)
    keep = lax.dynamic_slice_in_dim(both, core * tokens, tokens, axis=0)
    give = lax.dynamic_slice_in_dim(both, (1 - core) * tokens, tokens, axis=0)
    keep = keep + swap_core(give)
    keep = jnp.sum(spread(keep.astype(bf16), "y", 4).astype(f32), axis=0)
    give = swap_core(keep)
    write_sum = jnp.where(core == 0, keep, give)
    read_sum = jnp.where(core == 0, give, keep)

    terms = (grad * core_y - head_x * core_grad).reshape(tokens, heads, head_width)
    decay_part = jnp.sum(terms, axis=2).T
    local_tail = jnp.flip(jnp.cumsum(jnp.flip(decay_part, 1), axis=1), 1)
    end_state = start.reshape(heads, -1) * jnp.exp(last_sum) + local_state.reshape(
        heads, -1
    )
    above = jnp.sum(end_state * end.reshape(heads, -1), axis=1)
    decay_grad = local_tail + above[:, None]

    skip_part = jnp.sum((grad * head_x).reshape(tokens, heads, head_width), axis=(0, 2))
    square_part = jnp.sum((weight_grad * weight_grad).reshape(-1, heads, head_width), axis=(0, 2))
    small = jnp.concatenate([skip_part, square_part, jnp.zeros((112,), f32)])
    small = spread(jnp.broadcast_to(small[None], (8, 128)), CTX, BLOCKS)
    small = jnp.sum(small, axis=0)[0]
    skip_total, square_total = small[:heads], small[heads : 2 * heads]
    mean_square = square_total / float(WIDTH * head_width)
    new_second = beta_two * squared_average + (1.0 - beta_two) * mean_square
    new_first = beta_one * first_moment + (1.0 - beta_one) * weight_grad
    scale = jnp.repeat(jnp.sqrt(new_second / bias_two) + adam_eps, head_width)
    new_master = out_master - learn_rate * (
        new_first / bias_one / scale[None, :] + decoupled_decay * out_master
    )
    return (
        input_grad,
        write_sum,
        read_sum,
        decay_grad,
        skip_total,
        new_master,
        new_first,
        new_second,
    )


def solution(mesh):
    fine = Mesh(mesh.devices.reshape(4, 8, 4, 2), ("x", "z", "y", "core"))
    in_specs = (
        P(CTX, TP),
        P(CTX, None),
        P(CTX, None),
        P(TP, CTX),
        P(TP),
        P(CTX, None),
        P(CTX, TP),
        P(CTX, TP),
        P(TP),
    )
    out_specs = (
        P(CTX, TP),
        P(CTX, None),
        P(CTX, None),
        P(TP, CTX),
        P(TP),
        P(CTX, TP),
        P(CTX, TP),
        P(TP),
    )
    return jax.shard_map(shards, mesh=fine, in_specs=in_specs, out_specs=out_specs, check_vma=False)
```

```python
import jax
import jax.numpy as jnp
from jax import lax
from jax.experimental import pallas as pl
from jax.experimental.pallas import tpu as pltpu
from jax.sharding import Mesh, PartitionSpec as P

WIDTH = 4096
beta_one = 0.9
beta_two = 0.95
learn_rate = 0.004
decoupled_decay = 0.1
adam_eps = 1e-08
bias_one = 0.9999734386011124
bias_two = 0.994079470779666

f32 = jnp.float32
bf16 = jnp.bfloat16
CTX = ("x", "z")
TP = ("y", "core")
BLOCKS = 32


def mm(a, b, dims):
    return lax.dot_general(a, b, (dims, ((), ())), preferred_element_type=f32)


def block_weights(logs):
    i = lax.broadcasted_iota(jnp.int32, (BLOCKS, BLOCKS, BLOCKS), 0)
    j = lax.broadcasted_iota(jnp.int32, (BLOCKS, BLOCKS, BLOCKS), 1)
    r = lax.broadcasted_iota(jnp.int32, (BLOCKS, BLOCKS, BLOCKS), 2)
    between = jnp.sum(jnp.where((r > j) & (r < i), logs[None, None, :], 0.0), axis=2)
    rows = lax.broadcasted_iota(jnp.int32, (BLOCKS, BLOCKS), 0)
    cols = lax.broadcasted_iota(jnp.int32, (BLOCKS, BLOCKS), 1)
    return jnp.where(rows > cols, jnp.exp(between), 0.0)


def exact(a, b, dims):
    return lax.dot_general(
        a.astype(f32),
        b.astype(f32),
        (dims, ((), ())),
        precision=lax.Precision.HIGHEST,
        preferred_element_type=f32,
    )


def swap(value, axes):
    return lax.all_to_all(value, axes, 0, 0, tiled=True)


def swap_core(value):
    return lax.ppermute(value, "core", [(0, 1), (1, 0)])


def ring_shift(value, step):
    return lax.ppermute(value, "x", [(i, (i + step) % 4) for i in range(4)]) if step else value


def spread(value, axis, count):
    return swap(jnp.broadcast_to(value[None], (count,) + value.shape), axis)


TILE = 256
ANYWHERE = pl.BlockSpec(memory_space=pl.ANY)
IN_SMEM = pl.BlockSpec(memory_space=pltpu.SMEM)
IN_VMEM = pl.BlockSpec(memory_space=pltpu.VMEM)


def tile_of(j):
    return pl.ds(pl.multiple_of(j * TILE, TILE), TILE)


def fetch(refs, buffers, sems):
    copies = [
        pltpu.make_async_copy(ref, buffer, sems.at[i])
        for i, (ref, buffer) in enumerate(zip(refs, buffers))
    ]
    for copy in copies:
        copy.start()
    return copies


def like(arrays):
    return [pltpu.VMEM(a.shape, a.dtype) for a in arrays] + [pltpu.SemaphoreType.DMA((len(arrays),))]


def ring_grad_kernel(core_ref, own_in, other_in, weight_in, out_ref, own_ref, other_ref, weight_ref, sems):
    copies = fetch((weight_in, own_in, other_in), (weight_ref, own_ref, other_ref), sems)
    half = own_ref.shape[0]
    core = core_ref[0]
    copies[0].wait()
    for copy, ref, at in zip(copies[1:], (own_ref, other_ref), (core, 1 - core)):
        copy.wait()
        out_ref[pl.ds(pl.multiple_of(at * half, half), half), :] = jnp.dot(
            ref[...], weight_ref[...], preferred_element_type=f32
        ).astype(bf16)


def ring_grad_part(core, own, other, weight_rows):
    half, quarter = own.shape
    width = weight_rows.shape[1]
    return pl.pallas_call(
        ring_grad_kernel,
        out_shape=jax.ShapeDtypeStruct((2 * half, width), bf16),
        in_specs=[IN_SMEM] + [ANYWHERE] * 3,
        out_specs=IN_VMEM,
        scratch_shapes=like((own, other, weight_rows)),
        cost_estimate=pl.CostEstimate(
            flops=4 * half * quarter * width, bytes_accessed=3 << 20, transcendentals=0
        ),
        compiler_params=pltpu.CompilerParams(vmem_limit_bytes=16 << 20),
        name="ring_grad",
    )(core, own, other, weight_rows)


def weight_grad_kernel(core_ref, *refs):
    out_ref, sems = refs[12], refs[25]
    for copy in fetch(refs[:12], refs[13:25], sems):
        copy.wait()
    owns, others, ys = refs[13:17], refs[17:21], refs[21:25]
    half = owns[0].shape[0]
    core = core_ref[0]

    @pl.loop(0, out_ref.shape[0] // TILE)
    def _(j):
        total = None
        for own, other, y in zip(owns, others, ys):
            for ref, at in ((own, core), (other, 1 - core)):
                part = lax.dot_general(
                    ref[:, tile_of(j)],
                    y[pl.ds(pl.multiple_of(at * half, half), half), :],
                    (((0,), (0,)), ((), ())),
                    preferred_element_type=f32,
                )
                total = part if total is None else total + part
        out_ref[tile_of(j), :] = total.astype(bf16)


def weight_grad_part(core, owns, others, ys):
    half, quarter = owns[0].shape
    width = ys[0].shape[1]
    return pl.pallas_call(
        weight_grad_kernel,
        out_shape=jax.ShapeDtypeStruct((quarter, width), bf16),
        in_specs=[IN_SMEM] + [ANYWHERE] * 12,
        out_specs=IN_VMEM,
        scratch_shapes=like((*owns, *others, *ys)),
        cost_estimate=pl.CostEstimate(
            flops=16 * half * quarter * width, bytes_accessed=8 << 20, transcendentals=0
        ),
        compiler_params=pltpu.CompilerParams(vmem_limit_bytes=24 << 20),
        name="weight_grad",
    )(core, *owns, *others, *ys)


def chain(weights, parts, reverse):
    dims = ((0,), (0,)) if reverse else ((1,), (0,))
    out = exact(weights, parts.reshape(BLOCKS, 16 * 128), dims)
    return out.reshape(BLOCKS, 16, 128)


def shards(
    head_input,
    write_vector,
    read_vector,
    log_decay,
    skip_gain,
    out_grad,
    out_master,
    first_moment,
    squared_average,
):
    tokens, width = head_input.shape
    heads = log_decay.shape[0]
    head_width = width // heads

    core = lax.axis_index("core")
    ring = lax.axis_index("x")
    half = tokens // 2
    quarter = WIDTH // 4

    weight_rows = lax.all_gather(out_master.astype(bf16), "z", axis=0, tiled=True)
    owns = []
    for step in range(4):
        to = lax.rem(ring + step, 4)
        piece = lax.dynamic_slice(out_grad, (core * half, to * quarter), (half, quarter))
        owns.append(ring_shift(piece, step))

    running = jnp.cumsum(log_decay, axis=1)
    last_sum = running[:, -1:]
    gap = running[:, :, None] - running[:, None, :]
    row_index = lax.broadcasted_iota(jnp.int32, gap.shape, 1)
    col_index = lax.broadcasted_iota(jnp.int32, gap.shape, 2)
    lower_decay = jnp.exp(jnp.where(row_index >= col_index, gap, -1e30))
    to_end = jnp.exp(last_sum - running)
    from_start = jnp.exp(running)
    to_end_wide = jnp.repeat(to_end.T, head_width, axis=1)
    from_start_wide = jnp.repeat(from_start.T, head_width, axis=1)
    skip_wide = jnp.repeat(skip_gain, head_width)[None, :]

    head_x = head_input.astype(f32)
    x_decayed = head_x * to_end_wide
    local_state = exact(x_decayed, write_vector, ((0,), (0,)))
    totals = jnp.broadcast_to(last_sum[:, None, :, None], (heads, BLOCKS // heads, 8, 128))
    packed = jnp.concatenate(
        [local_state.reshape(BLOCKS, 16, 128), totals.reshape(BLOCKS, 8, 128)], axis=1
    )
    packed, owns[1] = lax.optimization_barrier((packed, owns[1]))
    packed = swap(packed, CTX)
    weights = block_weights(packed[:, 16, 0])
    start = chain(weights, packed[:, :16], False)
    start, weight_rows, owns = lax.optimization_barrier((start, weight_rows, owns))
    start = swap(start, CTX).reshape(width, 128)

    scores = mm(read_vector, write_vector, ((1,), (1,)))
    mixed = (lower_decay * scores[None]).astype(bf16)
    x_heads = head_input.reshape(tokens, heads, head_width)
    inner = jnp.einsum("hts,shp->thp", mixed, x_heads, preferred_element_type=f32)
    core_y = inner.reshape(tokens, width) + exact(read_vector, start, ((1,), (1,))) * from_start_wide
    out_y = (core_y + skip_wide * head_x).astype(bf16)

    others = [swap_core(piece) for piece in owns]
    core_one = jnp.full((1,), core, jnp.int32)
    parts = [
        ring_shift(ring_grad_part(core_one, owns[step], others[step], weight_rows), 4 - step)
        for step in (2, 1, 3)
    ]
    parts.append(ring_grad_part(core_one, owns[0], others[0], weight_rows))
    ring_y = [ring_shift(out_y, step) for step in range(4)]
    parts, _ = lax.optimization_barrier((parts, out_y))
    grad_low = sum(part.astype(f32) for part in parts).astype(bf16)

    partial = weight_grad_part(core_one, owns, others, ring_y)
    weight_grad = lax.psum_scatter(partial, "z", scatter_dimension=0, tiled=True).astype(f32)

    grad = grad_low.astype(f32)
    grad_decayed = grad * from_start_wide
    carried = exact(grad_decayed, read_vector, ((0,), (0,)))
    carried = swap(carried.reshape(BLOCKS, 16, 128), CTX)
    end = swap(chain(weights, carried, True), CTX).reshape(width, 128)

    grad_heads = grad_low.reshape(tokens, heads, head_width)
    inner = jnp.einsum("hst,shp->thp", mixed, grad_heads, preferred_element_type=f32)
    core_grad = inner.reshape(tokens, width) + exact(write_vector, end, ((1,), (1,))) * to_end_wide
    input_grad = (core_grad + skip_wide * grad).astype(bf16)
    cross_dots = jnp.einsum("thp,shp->hts", grad_heads, x_heads, preferred_element_type=f32)
    pair_weights = jnp.sum(lower_decay * cross_dots, axis=0).astype(bf16)
    read_grad = mm(pair_weights, write_vector, ((1,), (0,))) + mm(
        grad_decayed.astype(bf16), start.astype(bf16), ((1,), (0,))
    )
    write_grad = mm(pair_weights, read_vector, ((0,), (0,))) + mm(
        x_decayed.astype(bf16), end.astype(bf16), ((1,), (0,))
    )
    terms = (grad * core_y - head_x * core_grad).reshape(tokens, heads, head_width)
    decay_part = jnp.sum(terms, axis=2).T
    local_tail = jnp.flip(jnp.cumsum(jnp.flip(decay_part, 1), axis=1), 1)
    end_state = start.reshape(heads, -1) * jnp.exp(last_sum) + local_state.reshape(
        heads, -1
    )
    above = jnp.sum(end_state * end.reshape(heads, -1), axis=1)
    decay_grad = local_tail + above[:, None]

    skip_part = jnp.sum((grad * head_x).reshape(tokens, heads, head_width), axis=(0, 2))
    square_part = jnp.sum((weight_grad * weight_grad).reshape(-1, heads, head_width), axis=(0, 2))
    small = jnp.concatenate([skip_part, square_part, jnp.zeros((112,), f32)])
    small = spread(jnp.broadcast_to(small[None], (8, 128)), CTX, BLOCKS)
    small = jnp.sum(small, axis=0)[0]

    both = jnp.concatenate([write_grad, read_grad], axis=0)
    both, small = lax.optimization_barrier((both, small))
    keep = lax.dynamic_slice_in_dim(both, core * tokens, tokens, axis=0)
    give = lax.dynamic_slice_in_dim(both, (1 - core) * tokens, tokens, axis=0)
    keep = keep + swap_core(give)
    keep = jnp.sum(spread(keep.astype(bf16), "y", 4).astype(f32), axis=0)
    give = swap_core(keep)
    write_sum = jnp.where(core == 0, keep, give)
    read_sum = jnp.where(core == 0, give, keep)

    skip_total, square_total = small[:heads], small[heads : 2 * heads]
    mean_square = square_total / float(WIDTH * head_width)
    new_second = beta_two * squared_average + (1.0 - beta_two) * mean_square
    new_first = beta_one * first_moment + (1.0 - beta_one) * weight_grad
    scale = jnp.repeat(jnp.sqrt(new_second / bias_two) + adam_eps, head_width)
    new_master = out_master - learn_rate * (
        new_first / bias_one / scale[None, :] + decoupled_decay * out_master
    )
    return (
        input_grad,
        write_sum,
        read_sum,
        decay_grad,
        skip_total,
        new_master,
        new_first,
        new_second,
    )


def solution(mesh):
    fine = Mesh(mesh.devices.reshape(4, 8, 4, 2), ("x", "z", "y", "core"))
    in_specs = (
        P(CTX, TP),
        P(CTX, None),
        P(CTX, None),
        P(TP, CTX),
        P(TP),
        P(CTX, None),
        P(CTX, TP),
        P(CTX, TP),
        P(TP),
    )
    out_specs = (
        P(CTX, TP),
        P(CTX, None),
        P(CTX, None),
        P(TP, CTX),
        P(TP),
        P(CTX, TP),
        P(CTX, TP),
        P(TP),
    )
    return jax.shard_map(shards, mesh=fine, in_specs=in_specs, out_specs=out_specs, check_vma=False)
```

```python
import jax
import jax.numpy as jnp
from jax import lax
from jax.experimental import pallas as pl
from jax.experimental.pallas import tpu as pltpu
from jax.sharding import Mesh, PartitionSpec as P

WIDTH = 4096
beta_one = 0.9
beta_two = 0.95
learn_rate = 0.004
decoupled_decay = 0.1
adam_eps = 1e-08
bias_one = 0.9999734386011124
bias_two = 0.994079470779666

f32 = jnp.float32
bf16 = jnp.bfloat16
CTX = ("x", "z")
TP = ("y", "core")
BLOCKS = 32


def mm(a, b, dims):
    return lax.dot_general(a, b, (dims, ((), ())), preferred_element_type=f32)


def block_weights(logs):
    i = lax.broadcasted_iota(jnp.int32, (BLOCKS, BLOCKS, BLOCKS), 0)
    j = lax.broadcasted_iota(jnp.int32, (BLOCKS, BLOCKS, BLOCKS), 1)
    r = lax.broadcasted_iota(jnp.int32, (BLOCKS, BLOCKS, BLOCKS), 2)
    between = jnp.sum(jnp.where((r > j) & (r < i), logs[None, None, :], 0.0), axis=2)
    rows = lax.broadcasted_iota(jnp.int32, (BLOCKS, BLOCKS), 0)
    cols = lax.broadcasted_iota(jnp.int32, (BLOCKS, BLOCKS), 1)
    return jnp.where(rows > cols, jnp.exp(between), 0.0)


def exact(a, b, dims):
    return lax.dot_general(
        a.astype(f32),
        b.astype(f32),
        (dims, ((), ())),
        precision=lax.Precision.HIGHEST,
        preferred_element_type=f32,
    )


def swap(value, axes):
    return lax.all_to_all(value, axes, 0, 0, tiled=True)


def swap_core(value):
    return lax.ppermute(value, "core", [(0, 1), (1, 0)])


def ring_shift(value, step):
    return lax.ppermute(value, "x", [(i, (i + step) % 4) for i in range(4)]) if step else value


def spread(value, axis, count):
    return swap(jnp.broadcast_to(value[None], (count,) + value.shape), axis)


TILE = 256
ANYWHERE = pl.BlockSpec(memory_space=pl.ANY)
IN_SMEM = pl.BlockSpec(memory_space=pltpu.SMEM)
IN_VMEM = pl.BlockSpec(memory_space=pltpu.VMEM)


def tile_of(j):
    return pl.ds(pl.multiple_of(j * TILE, TILE), TILE)


def fetch(refs, buffers, sems):
    copies = [
        pltpu.make_async_copy(ref, buffer, sems.at[i])
        for i, (ref, buffer) in enumerate(zip(refs, buffers))
    ]
    for copy in copies:
        copy.start()
    return copies


def like(arrays):
    return [pltpu.VMEM(a.shape, a.dtype) for a in arrays] + [pltpu.SemaphoreType.DMA((len(arrays),))]


def ring_grad_kernel(core_ref, own_in, other_in, weight_in, out_ref, own_ref, other_ref, weight_ref, sems):
    copies = fetch((weight_in, own_in, other_in), (weight_ref, own_ref, other_ref), sems)
    half = own_ref.shape[0]
    core = core_ref[0]
    copies[0].wait()
    for copy, ref, at in zip(copies[1:], (own_ref, other_ref), (core, 1 - core)):
        copy.wait()
        out_ref[pl.ds(pl.multiple_of(at * half, half), half), :] = jnp.dot(
            ref[...], weight_ref[...], preferred_element_type=f32
        ).astype(bf16)


def ring_grad_part(core, own, other, weight_rows):
    half, quarter = own.shape
    width = weight_rows.shape[1]
    return pl.pallas_call(
        ring_grad_kernel,
        out_shape=jax.ShapeDtypeStruct((2 * half, width), bf16),
        in_specs=[IN_SMEM] + [ANYWHERE] * 3,
        out_specs=IN_VMEM,
        scratch_shapes=like((own, other, weight_rows)),
        cost_estimate=pl.CostEstimate(
            flops=4 * half * quarter * width, bytes_accessed=3 << 20, transcendentals=0
        ),
        compiler_params=pltpu.CompilerParams(vmem_limit_bytes=16 << 20),
        name="ring_grad",
    )(core, own, other, weight_rows)


def weight_grad_kernel(core_ref, *refs):
    out_ref, sems = refs[12], refs[25]
    for copy in fetch(refs[:12], refs[13:25], sems):
        copy.wait()
    owns, others, ys = refs[13:17], refs[17:21], refs[21:25]
    half = owns[0].shape[0]
    core = core_ref[0]

    @pl.loop(0, out_ref.shape[0] // TILE)
    def _(j):
        total = None
        for own, other, y in zip(owns, others, ys):
            for ref, at in ((own, core), (other, 1 - core)):
                part = lax.dot_general(
                    ref[:, tile_of(j)],
                    y[pl.ds(pl.multiple_of(at * half, half), half), :],
                    (((0,), (0,)), ((), ())),
                    preferred_element_type=f32,
                )
                total = part if total is None else total + part
        out_ref[tile_of(j), :] = total.astype(bf16)


def weight_grad_part(core, owns, others, ys):
    half, quarter = owns[0].shape
    width = ys[0].shape[1]
    return pl.pallas_call(
        weight_grad_kernel,
        out_shape=jax.ShapeDtypeStruct((quarter, width), bf16),
        in_specs=[IN_SMEM] + [ANYWHERE] * 12,
        out_specs=IN_VMEM,
        scratch_shapes=like((*owns, *others, *ys)),
        cost_estimate=pl.CostEstimate(
            flops=16 * half * quarter * width, bytes_accessed=8 << 20, transcendentals=0
        ),
        compiler_params=pltpu.CompilerParams(vmem_limit_bytes=24 << 20),
        name="weight_grad",
    )(core, *owns, *others, *ys)


def chain(weights, parts, reverse):
    dims = ((0,), (0,)) if reverse else ((1,), (0,))
    out = exact(weights, parts.reshape(BLOCKS, 16 * 128), dims)
    return out.reshape(BLOCKS, 16, 128)


def shards(
    head_input,
    write_vector,
    read_vector,
    log_decay,
    skip_gain,
    out_grad,
    out_master,
    first_moment,
    squared_average,
):
    tokens, width = head_input.shape
    heads = log_decay.shape[0]
    head_width = width // heads

    core = lax.axis_index("core")
    ring = lax.axis_index("x")
    half = tokens // 2
    quarter = WIDTH // 4

    weight_rows = lax.all_gather(out_master.astype(bf16), "z", axis=0, tiled=True)
    def piece(step, start, rows):
        to = lax.rem(ring + step, 4)
        return lax.dynamic_slice(out_grad, (core * half + start, to * quarter), (rows, quarter))

    near = half // 2
    up = ring_shift(jnp.concatenate([piece(1, 0, half), piece(2, 0, near)]), 1)
    down = ring_shift(jnp.concatenate([piece(3, 0, half), piece(2, near, near)]), 3)

    running = jnp.cumsum(log_decay, axis=1)
    last_sum = running[:, -1:]
    gap = running[:, :, None] - running[:, None, :]
    row_index = lax.broadcasted_iota(jnp.int32, gap.shape, 1)
    col_index = lax.broadcasted_iota(jnp.int32, gap.shape, 2)
    lower_decay = jnp.exp(jnp.where(row_index >= col_index, gap, -1e30))
    to_end = jnp.exp(last_sum - running)
    from_start = jnp.exp(running)
    to_end_wide = jnp.repeat(to_end.T, head_width, axis=1)
    from_start_wide = jnp.repeat(from_start.T, head_width, axis=1)
    skip_wide = jnp.repeat(skip_gain, head_width)[None, :]

    head_x = head_input.astype(f32)
    x_decayed = head_x * to_end_wide
    local_state = exact(x_decayed, write_vector, ((0,), (0,)))
    totals = jnp.broadcast_to(last_sum[:, None, :, None], (heads, BLOCKS // heads, 8, 128))
    packed = jnp.concatenate(
        [local_state.reshape(BLOCKS, 16, 128), totals.reshape(BLOCKS, 8, 128)], axis=1
    )
    packed, up, down = lax.optimization_barrier((packed, up, down))
    far = jnp.concatenate([ring_shift(up[half:], 1), ring_shift(down[half:], 3)])
    owns = [piece(0, 0, half), up[:half], far, down[:half]]
    packed = swap(packed, CTX)
    weights = block_weights(packed[:, 16, 0])
    start = swap(chain(weights, packed[:, :16], False), CTX).reshape(width, 128)
    others = [swap_core(piece) for piece in owns]
    start, weight_rows = lax.optimization_barrier((start, weight_rows))

    scores = mm(read_vector, write_vector, ((1,), (1,)))
    mixed = (lower_decay * scores[None]).astype(bf16)
    x_heads = head_input.reshape(tokens, heads, head_width)
    inner = jnp.einsum("hts,shp->thp", mixed, x_heads, preferred_element_type=f32)
    core_y = inner.reshape(tokens, width) + exact(read_vector, start, ((1,), (1,))) * from_start_wide
    out_y = (core_y + skip_wide * head_x).astype(bf16)

    core_one = jnp.full((1,), core, jnp.int32)
    part_far, part_down, part_up, part_own = (
        ring_grad_part(core_one, owns[step], others[step], weight_rows) for step in (2, 3, 1, 0)
    )
    from_up = ring_shift(part_far[:half], 1).astype(f32) + part_down[:half].astype(f32)
    from_down = ring_shift(part_far[half:], 3).astype(f32) + part_up[half:].astype(f32)
    parts = [
        part_own,
        ring_shift(jnp.concatenate([from_up.astype(bf16), part_down[half:]]), 1),
        ring_shift(jnp.concatenate([part_up[:half], from_down.astype(bf16)]), 3),
    ]
    y_up, y_down = ring_shift(out_y, 1), ring_shift(out_y, 3)
    y_far = jnp.concatenate([ring_shift(y_up[:half], 1), ring_shift(y_down[half:], 3)])
    ring_y = [out_y, y_up, y_far, y_down]
    parts, _ = lax.optimization_barrier((parts, out_y))
    grad_low = sum(part.astype(f32) for part in parts).astype(bf16)

    partial = weight_grad_part(core_one, owns, others, ring_y)
    weight_grad = lax.psum_scatter(partial, "z", scatter_dimension=0, tiled=True).astype(f32)

    grad = grad_low.astype(f32)
    grad_decayed = grad * from_start_wide
    carried = exact(grad_decayed, read_vector, ((0,), (0,)))
    carried = swap(carried.reshape(BLOCKS, 16, 128), CTX)
    end = swap(chain(weights, carried, True), CTX).reshape(width, 128)

    grad_heads = grad_low.reshape(tokens, heads, head_width)
    inner = jnp.einsum("hst,shp->thp", mixed, grad_heads, preferred_element_type=f32)
    cross_dots = jnp.einsum("thp,shp->hts", grad_heads, x_heads, preferred_element_type=f32)
    pair_weights = jnp.sum(lower_decay * cross_dots, axis=0).astype(bf16)
    read_grad = mm(pair_weights, write_vector, ((1,), (0,))) + mm(
        grad_decayed.astype(bf16), start.astype(bf16), ((1,), (0,))
    )
    write_grad = mm(pair_weights, read_vector, ((0,), (0,))) + mm(
        x_decayed.astype(bf16), end.astype(bf16), ((1,), (0,))
    )

    both = jnp.concatenate([write_grad, read_grad], axis=0)
    both, end = lax.optimization_barrier((both, end))
    keep = lax.dynamic_slice_in_dim(both, core * tokens, tokens, axis=0)
    give = lax.dynamic_slice_in_dim(both, (1 - core) * tokens, tokens, axis=0)
    mine = (keep + swap_core(give)).astype(bf16)
    column = lax.axis_index("y")
    terms = [mine] + [
        lax.ppermute(mine, "y", [(i, (i + step) % 4) for i in range(4)]) for step in range(1, 4)
    ]
    keep = 0.0
    for y in range(4):
        keep = keep + lax.select_n(lax.rem(column + 4 - y, 4), *terms).astype(f32)
    give = swap_core(keep)
    write_sum = jnp.where(core == 0, keep, give)
    read_sum = jnp.where(core == 0, give, keep)

    core_grad = inner.reshape(tokens, width) + exact(write_vector, end, ((1,), (1,))) * to_end_wide
    input_grad = (core_grad + skip_wide * grad).astype(bf16)

    terms = (grad * core_y - head_x * core_grad).reshape(tokens, heads, head_width)
    decay_part = jnp.sum(terms, axis=2).T
    local_tail = jnp.flip(jnp.cumsum(jnp.flip(decay_part, 1), axis=1), 1)
    end_state = start.reshape(heads, -1) * jnp.exp(last_sum) + local_state.reshape(
        heads, -1
    )
    above = jnp.sum(end_state * end.reshape(heads, -1), axis=1)
    decay_grad = local_tail + above[:, None]

    skip_part = jnp.sum((grad * head_x).reshape(tokens, heads, head_width), axis=(0, 2))
    square_part = jnp.sum((weight_grad * weight_grad).reshape(-1, heads, head_width), axis=(0, 2))
    small = jnp.concatenate([skip_part, square_part, jnp.zeros((112,), f32)])
    small = spread(jnp.broadcast_to(small[None], (8, 128)), CTX, BLOCKS)
    small = jnp.sum(small, axis=0)[0]

    skip_total, square_total = small[:heads], small[heads : 2 * heads]
    mean_square = square_total / float(WIDTH * head_width)
    new_second = beta_two * squared_average + (1.0 - beta_two) * mean_square
    new_first = beta_one * first_moment + (1.0 - beta_one) * weight_grad
    scale = jnp.repeat(jnp.sqrt(new_second / bias_two) + adam_eps, head_width)
    new_master = out_master - learn_rate * (
        new_first / bias_one / scale[None, :] + decoupled_decay * out_master
    )
    return (
        input_grad,
        write_sum,
        read_sum,
        decay_grad,
        skip_total,
        new_master,
        new_first,
        new_second,
    )


def solution(mesh):
    fine = Mesh(mesh.devices.reshape(4, 8, 4, 2), ("x", "z", "y", "core"))
    in_specs = (
        P(CTX, TP),
        P(CTX, None),
        P(CTX, None),
        P(TP, CTX),
        P(TP),
        P(CTX, None),
        P(CTX, TP),
        P(CTX, TP),
        P(TP),
    )
    out_specs = (
        P(CTX, TP),
        P(CTX, None),
        P(CTX, None),
        P(TP, CTX),
        P(TP),
        P(CTX, TP),
        P(CTX, TP),
        P(TP),
    )
    return jax.shard_map(shards, mesh=fine, in_specs=in_specs, out_specs=out_specs, check_vma=False)
```

```python
import jax
import jax.numpy as jnp
from jax import lax
from jax.experimental import pallas as pl
from jax.experimental.pallas import tpu as pltpu
from jax.sharding import Mesh, PartitionSpec as P

WIDTH = 4096
beta_one = 0.9
beta_two = 0.95
learn_rate = 0.004
decoupled_decay = 0.1
adam_eps = 1e-08
bias_one = 0.9999734386011124
bias_two = 0.994079470779666

f32 = jnp.float32
bf16 = jnp.bfloat16
CTX = ("x", "z")
TP = ("y", "core")
BLOCKS = 32


def mm(a, b, dims):
    return lax.dot_general(a, b, (dims, ((), ())), preferred_element_type=f32)


def block_weights(logs):
    i = lax.broadcasted_iota(jnp.int32, (BLOCKS, BLOCKS, BLOCKS), 0)
    j = lax.broadcasted_iota(jnp.int32, (BLOCKS, BLOCKS, BLOCKS), 1)
    r = lax.broadcasted_iota(jnp.int32, (BLOCKS, BLOCKS, BLOCKS), 2)
    between = jnp.sum(jnp.where((r > j) & (r < i), logs[None, None, :], 0.0), axis=2)
    rows = lax.broadcasted_iota(jnp.int32, (BLOCKS, BLOCKS), 0)
    cols = lax.broadcasted_iota(jnp.int32, (BLOCKS, BLOCKS), 1)
    return jnp.where(rows > cols, jnp.exp(between), 0.0)


def exact(a, b, dims):
    return lax.dot_general(
        a.astype(f32),
        b.astype(f32),
        (dims, ((), ())),
        precision=lax.Precision.HIGHEST,
        preferred_element_type=f32,
    )


def swap(value, axes):
    return lax.all_to_all(value, axes, 0, 0, tiled=True)


def swap_core(value):
    return lax.ppermute(value, "core", [(0, 1), (1, 0)])


def ring_shift(value, step):
    return lax.ppermute(value, "x", [(i, (i + step) % 4) for i in range(4)]) if step else value


def spread(value, axis, count):
    return swap(jnp.broadcast_to(value[None], (count,) + value.shape), axis)


TILE = 256
ANYWHERE = pl.BlockSpec(memory_space=pl.ANY)
IN_SMEM = pl.BlockSpec(memory_space=pltpu.SMEM)
IN_VMEM = pl.BlockSpec(memory_space=pltpu.VMEM)


def tile_of(j):
    return pl.ds(pl.multiple_of(j * TILE, TILE), TILE)


def fetch(refs, buffers, sems):
    copies = [
        pltpu.make_async_copy(ref, buffer, sems.at[i])
        for i, (ref, buffer) in enumerate(zip(refs, buffers))
    ]
    for copy in copies:
        copy.start()
    return copies


def like(arrays):
    return [pltpu.VMEM(a.shape, a.dtype) for a in arrays] + [pltpu.SemaphoreType.DMA((len(arrays),))]


def ring_grad_kernel(core_ref, own_in, other_in, weight_in, out_ref, own_ref, other_ref, weight_ref, sems):
    copies = fetch((weight_in, own_in, other_in), (weight_ref, own_ref, other_ref), sems)
    half = own_ref.shape[0]
    core = core_ref[0]
    copies[0].wait()
    for copy, ref, at in zip(copies[1:], (own_ref, other_ref), (core, 1 - core)):
        copy.wait()
        out_ref[pl.ds(pl.multiple_of(at * half, half), half), :] = jnp.dot(
            ref[...], weight_ref[...], preferred_element_type=f32
        ).astype(bf16)


def ring_grad_part(core, own, other, weight_rows):
    half, quarter = own.shape
    width = weight_rows.shape[1]
    return pl.pallas_call(
        ring_grad_kernel,
        out_shape=jax.ShapeDtypeStruct((2 * half, width), bf16),
        in_specs=[IN_SMEM] + [ANYWHERE] * 3,
        out_specs=IN_VMEM,
        scratch_shapes=like((own, other, weight_rows)),
        cost_estimate=pl.CostEstimate(
            flops=4 * half * quarter * width, bytes_accessed=3 << 20, transcendentals=0
        ),
        compiler_params=pltpu.CompilerParams(vmem_limit_bytes=16 << 20),
        name="ring_grad",
    )(core, own, other, weight_rows)


def weight_grad_kernel(core_ref, *refs):
    out_ref, sems = refs[12], refs[25]
    for copy in fetch(refs[:12], refs[13:25], sems):
        copy.wait()
    owns, others, ys = refs[13:17], refs[17:21], refs[21:25]
    half = owns[0].shape[0]
    core = core_ref[0]

    @pl.loop(0, out_ref.shape[0] // TILE)
    def _(j):
        total = None
        for own, other, y in zip(owns, others, ys):
            for ref, at in ((own, core), (other, 1 - core)):
                part = lax.dot_general(
                    ref[:, tile_of(j)],
                    y[pl.ds(pl.multiple_of(at * half, half), half), :],
                    (((0,), (0,)), ((), ())),
                    preferred_element_type=f32,
                )
                total = part if total is None else total + part
        out_ref[tile_of(j), :] = total.astype(bf16)


def weight_grad_part(core, owns, others, ys):
    half, quarter = owns[0].shape
    width = ys[0].shape[1]
    return pl.pallas_call(
        weight_grad_kernel,
        out_shape=jax.ShapeDtypeStruct((quarter, width), bf16),
        in_specs=[IN_SMEM] + [ANYWHERE] * 12,
        out_specs=IN_VMEM,
        scratch_shapes=like((*owns, *others, *ys)),
        cost_estimate=pl.CostEstimate(
            flops=16 * half * quarter * width, bytes_accessed=8 << 20, transcendentals=0
        ),
        compiler_params=pltpu.CompilerParams(vmem_limit_bytes=24 << 20),
        name="weight_grad",
    )(core, *owns, *others, *ys)


def chain(weights, parts, reverse):
    dims = ((0,), (0,)) if reverse else ((1,), (0,))
    out = exact(weights, parts.reshape(BLOCKS, 16 * 128), dims)
    return out.reshape(BLOCKS, 16, 128)


def shards(
    head_input,
    write_vector,
    read_vector,
    log_decay,
    skip_gain,
    out_grad,
    out_master,
    first_moment,
    squared_average,
):
    tokens, width = head_input.shape
    heads = log_decay.shape[0]
    head_width = width // heads

    core = lax.axis_index("core")
    ring = lax.axis_index("x")
    half = tokens // 2
    quarter = WIDTH // 4

    weight_rows = lax.all_gather(out_master.astype(bf16), "z", axis=0, tiled=True)
    owns = []
    for step in range(4):
        to = lax.rem(ring + step, 4)
        piece = lax.dynamic_slice(out_grad, (core * half, to * quarter), (half, quarter))
        owns.append(ring_shift(piece, step))

    running = jnp.cumsum(log_decay, axis=1)
    last_sum = running[:, -1:]
    gap = running[:, :, None] - running[:, None, :]
    row_index = lax.broadcasted_iota(jnp.int32, gap.shape, 1)
    col_index = lax.broadcasted_iota(jnp.int32, gap.shape, 2)
    lower_decay = jnp.exp(jnp.where(row_index >= col_index, gap, -1e30))
    to_end = jnp.exp(last_sum - running)
    from_start = jnp.exp(running)
    to_end_wide = jnp.repeat(to_end.T, head_width, axis=1)
    from_start_wide = jnp.repeat(from_start.T, head_width, axis=1)
    skip_wide = jnp.repeat(skip_gain, head_width)[None, :]

    head_x = head_input.astype(f32)
    x_decayed = head_x * to_end_wide
    local_state = exact(x_decayed, write_vector, ((0,), (0,)))
    totals = jnp.broadcast_to(last_sum[:, None, :, None], (heads, BLOCKS // heads, 8, 128))
    packed = jnp.concatenate(
        [local_state.reshape(BLOCKS, 16, 128), totals.reshape(BLOCKS, 8, 128)], axis=1
    )
    packed = swap(packed, CTX)
    weights = block_weights(packed[:, 16, 0])
    entering = chain(weights, packed[:, :16], False)
    start = swap(entering, CTX).reshape(width, 128)
    owns, _ = lax.optimization_barrier((owns, start))
    others = [swap_core(piece) for piece in owns]
    start, weight_rows = lax.optimization_barrier((start, weight_rows))

    scores = mm(read_vector, write_vector, ((1,), (1,)))
    mixed = (lower_decay * scores[None]).astype(bf16)
    x_heads = head_input.reshape(tokens, heads, head_width)
    inner = jnp.einsum("hts,shp->thp", mixed, x_heads, preferred_element_type=f32)
    core_y = inner.reshape(tokens, width) + exact(read_vector, start, ((1,), (1,))) * from_start_wide
    out_y = (core_y + skip_wide * head_x).astype(bf16)

    core_one = jnp.full((1,), core, jnp.int32)
    part_far, part_down, part_up, part_own = (
        ring_grad_part(core_one, owns[step], others[step], weight_rows) for step in (2, 3, 1, 0)
    )
    from_up = ring_shift(part_far[:half], 1).astype(f32) + part_down[:half].astype(f32)
    from_down = ring_shift(part_far[half:], 3).astype(f32) + part_up[half:].astype(f32)
    parts = [
        part_own,
        ring_shift(jnp.concatenate([from_up.astype(bf16), part_down[half:]]), 1),
        ring_shift(jnp.concatenate([part_up[:half], from_down.astype(bf16)]), 3),
    ]
    ring_y = [ring_shift(out_y, step) for step in range(4)]
    parts, _ = lax.optimization_barrier((parts, out_y))
    grad_low = sum(part.astype(f32) for part in parts).astype(bf16)

    partial = weight_grad_part(core_one, owns, others, ring_y)
    weight_grad = lax.psum_scatter(partial, "z", scatter_dimension=0, tiled=True).astype(f32)

    grad = grad_low.astype(f32)
    grad_decayed = grad * from_start_wide
    carried = exact(grad_decayed, read_vector, ((0,), (0,)))
    carried = swap(carried.reshape(BLOCKS, 16, 128), CTX)
    end = swap(chain(weights, carried, True), CTX).reshape(width, 128)

    grad_heads = grad_low.reshape(tokens, heads, head_width)
    inner = jnp.einsum("hst,shp->thp", mixed, grad_heads, preferred_element_type=f32)
    cross_dots = jnp.einsum("thp,shp->hts", grad_heads, x_heads, preferred_element_type=f32)
    pair_weights = jnp.sum(lower_decay * cross_dots, axis=0).astype(bf16)
    read_grad = mm(pair_weights, write_vector, ((1,), (0,))) + mm(
        grad_decayed.astype(bf16), start.astype(bf16), ((1,), (0,))
    )
    write_grad = mm(pair_weights, read_vector, ((0,), (0,))) + mm(
        x_decayed.astype(bf16), end.astype(bf16), ((1,), (0,))
    )

    skip_part = jnp.sum((grad * head_x).reshape(tokens, heads, head_width), axis=(0, 2))
    square_part = jnp.sum((weight_grad * weight_grad).reshape(-1, heads, head_width), axis=(0, 2))
    small = jnp.concatenate([skip_part, square_part, jnp.zeros((112,), f32)])

    both = jnp.concatenate([write_grad, read_grad], axis=0)
    keep = lax.dynamic_slice_in_dim(both, core * tokens, tokens, axis=0)
    give = lax.dynamic_slice_in_dim(both, (1 - core) * tokens, tokens, axis=0)
    mine = (keep + swap_core(give)).astype(bf16)
    mine, end, small = lax.optimization_barrier((mine, end, small))
    small = spread(jnp.broadcast_to(small[None], (8, 128)), CTX, BLOCKS)
    small = jnp.sum(small, axis=0)[0]
    column = lax.axis_index("y")
    terms = [mine] + [
        lax.ppermute(mine, "y", [(i, (i + step) % 4) for i in range(4)]) for step in range(1, 4)
    ]
    keep = 0.0
    for y in range(4):
        keep = keep + lax.select_n(lax.rem(column + 4 - y, 4), *terms).astype(f32)
    give = swap_core(keep)
    write_sum = jnp.where(core == 0, keep, give)
    read_sum = jnp.where(core == 0, give, keep)

    core_grad = inner.reshape(tokens, width) + exact(write_vector, end, ((1,), (1,))) * to_end_wide
    input_grad = (core_grad + skip_wide * grad).astype(bf16)

    terms = (grad * core_y - head_x * core_grad).reshape(tokens, heads, head_width)
    decay_part = jnp.sum(terms, axis=2).T
    local_tail = jnp.flip(jnp.cumsum(jnp.flip(decay_part, 1), axis=1), 1)
    end_state = start.reshape(heads, -1) * jnp.exp(last_sum) + local_state.reshape(
        heads, -1
    )
    above = jnp.sum(end_state * end.reshape(heads, -1), axis=1)
    decay_grad = local_tail + above[:, None]

    skip_total, square_total = small[:heads], small[heads : 2 * heads]
    mean_square = square_total / float(WIDTH * head_width)
    new_second = beta_two * squared_average + (1.0 - beta_two) * mean_square
    new_first = beta_one * first_moment + (1.0 - beta_one) * weight_grad
    scale = jnp.repeat(jnp.sqrt(new_second / bias_two) + adam_eps, head_width)
    new_master = out_master - learn_rate * (
        new_first / bias_one / scale[None, :] + decoupled_decay * out_master
    )
    return (
        input_grad,
        write_sum,
        read_sum,
        decay_grad,
        skip_total,
        new_master,
        new_first,
        new_second,
    )


def solution(mesh):
    fine = Mesh(mesh.devices.reshape(4, 8, 4, 2), ("x", "z", "y", "core"))
    in_specs = (
        P(CTX, TP),
        P(CTX, None),
        P(CTX, None),
        P(TP, CTX),
        P(TP),
        P(CTX, None),
        P(CTX, TP),
        P(CTX, TP),
        P(TP),
    )
    out_specs = (
        P(CTX, TP),
        P(CTX, None),
        P(CTX, None),
        P(TP, CTX),
        P(TP),
        P(CTX, TP),
        P(CTX, TP),
        P(TP),
    )
    return jax.shard_map(shards, mesh=fine, in_specs=in_specs, out_specs=out_specs, check_vma=False)
```

```python
import jax
import jax.numpy as jnp
from jax import lax
from jax.experimental import pallas as pl
from jax.experimental.pallas import tpu as pltpu
from jax.sharding import Mesh, PartitionSpec as P

WIDTH = 4096
beta_one = 0.9
beta_two = 0.95
learn_rate = 0.004
decoupled_decay = 0.1
adam_eps = 1e-08
bias_one = 0.9999734386011124
bias_two = 0.994079470779666

f32 = jnp.float32
bf16 = jnp.bfloat16
CTX = ("x", "z")
TP = ("y", "core")
BLOCKS = 32


def mm(a, b, dims):
    return lax.dot_general(a, b, (dims, ((), ())), preferred_element_type=f32)


def block_weights(logs):
    i = lax.broadcasted_iota(jnp.int32, (BLOCKS, BLOCKS, BLOCKS), 0)
    j = lax.broadcasted_iota(jnp.int32, (BLOCKS, BLOCKS, BLOCKS), 1)
    r = lax.broadcasted_iota(jnp.int32, (BLOCKS, BLOCKS, BLOCKS), 2)
    between = jnp.sum(jnp.where((r > j) & (r < i), logs[None, None, :], 0.0), axis=2)
    rows = lax.broadcasted_iota(jnp.int32, (BLOCKS, BLOCKS), 0)
    cols = lax.broadcasted_iota(jnp.int32, (BLOCKS, BLOCKS), 1)
    return jnp.where(rows > cols, jnp.exp(between), 0.0)


def exact(a, b, dims):
    return lax.dot_general(
        a.astype(f32),
        b.astype(f32),
        (dims, ((), ())),
        precision=lax.Precision.HIGHEST,
        preferred_element_type=f32,
    )


def swap(value, axes):
    return lax.all_to_all(value, axes, 0, 0, tiled=True)


def swap_core(value):
    return lax.ppermute(value, "core", [(0, 1), (1, 0)])


def ring_shift(value, step):
    return lax.ppermute(value, "x", [(i, (i + step) % 4) for i in range(4)]) if step else value


def spread(value, axis, count):
    return swap(jnp.broadcast_to(value[None], (count,) + value.shape), axis)


TILE = 256
ANYWHERE = pl.BlockSpec(memory_space=pl.ANY)
IN_SMEM = pl.BlockSpec(memory_space=pltpu.SMEM)
IN_VMEM = pl.BlockSpec(memory_space=pltpu.VMEM)


def tile_of(j):
    return pl.ds(pl.multiple_of(j * TILE, TILE), TILE)


def fetch(refs, buffers, sems):
    copies = [
        pltpu.make_async_copy(ref, buffer, sems.at[i])
        for i, (ref, buffer) in enumerate(zip(refs, buffers))
    ]
    for copy in copies:
        copy.start()
    return copies


def like(arrays):
    return [pltpu.VMEM(a.shape, a.dtype) for a in arrays] + [pltpu.SemaphoreType.DMA((len(arrays),))]


def ring_grad_kernel(core_ref, own_in, other_in, weight_in, out_ref, own_ref, other_ref, weight_ref, sems):
    copies = fetch((weight_in, own_in, other_in), (weight_ref, own_ref, other_ref), sems)
    half = own_ref.shape[0]
    core = core_ref[0]
    copies[0].wait()
    for copy, ref, at in zip(copies[1:], (own_ref, other_ref), (core, 1 - core)):
        copy.wait()
        out_ref[pl.ds(pl.multiple_of(at * half, half), half), :] = jnp.dot(
            ref[...], weight_ref[...], preferred_element_type=f32
        ).astype(bf16)


def ring_grad_part(core, own, other, weight_rows):
    half, quarter = own.shape
    width = weight_rows.shape[1]
    return pl.pallas_call(
        ring_grad_kernel,
        out_shape=jax.ShapeDtypeStruct((2 * half, width), bf16),
        in_specs=[IN_SMEM] + [ANYWHERE] * 3,
        out_specs=IN_VMEM,
        scratch_shapes=like((own, other, weight_rows)),
        cost_estimate=pl.CostEstimate(
            flops=4 * half * quarter * width, bytes_accessed=3 << 20, transcendentals=0
        ),
        compiler_params=pltpu.CompilerParams(vmem_limit_bytes=16 << 20),
        name="ring_grad",
    )(core, own, other, weight_rows)


def weight_grad_kernel(core_ref, *refs):
    out_ref, sems = refs[12], refs[25]
    for copy in fetch(refs[:12], refs[13:25], sems):
        copy.wait()
    owns, others, ys = refs[13:17], refs[17:21], refs[21:25]
    half = owns[0].shape[0]
    core = core_ref[0]

    @pl.loop(0, out_ref.shape[0] // TILE)
    def _(j):
        total = None
        for own, other, y in zip(owns, others, ys):
            for ref, at in ((own, core), (other, 1 - core)):
                part = lax.dot_general(
                    ref[:, tile_of(j)],
                    y[pl.ds(pl.multiple_of(at * half, half), half), :],
                    (((0,), (0,)), ((), ())),
                    preferred_element_type=f32,
                )
                total = part if total is None else total + part
        out_ref[tile_of(j), :] = total.astype(bf16)


def weight_grad_part(core, owns, others, ys):
    half, quarter = owns[0].shape
    width = ys[0].shape[1]
    return pl.pallas_call(
        weight_grad_kernel,
        out_shape=jax.ShapeDtypeStruct((quarter, width), bf16),
        in_specs=[IN_SMEM] + [ANYWHERE] * 12,
        out_specs=IN_VMEM,
        scratch_shapes=like((*owns, *others, *ys)),
        cost_estimate=pl.CostEstimate(
            flops=16 * half * quarter * width, bytes_accessed=8 << 20, transcendentals=0
        ),
        compiler_params=pltpu.CompilerParams(vmem_limit_bytes=24 << 20),
        name="weight_grad",
    )(core, *owns, *others, *ys)


def chain(weights, parts, reverse):
    dims = ((0,), (0,)) if reverse else ((1,), (0,))
    out = exact(weights, parts.reshape(BLOCKS, 16 * 128), dims)
    return out.reshape(BLOCKS, 16, 128)


def shards(
    head_input,
    write_vector,
    read_vector,
    log_decay,
    skip_gain,
    out_grad,
    out_master,
    first_moment,
    squared_average,
):
    tokens, width = head_input.shape
    heads = log_decay.shape[0]
    head_width = width // heads

    core = lax.axis_index("core")
    ring = lax.axis_index("x")
    half = tokens // 2
    quarter = WIDTH // 4

    weight_rows = lax.all_gather(out_master.astype(bf16), "z", axis=0, tiled=True)
    owns = []
    for step in range(4):
        to = lax.rem(ring + step, 4)
        piece = lax.dynamic_slice(out_grad, (core * half, to * quarter), (half, quarter))
        owns.append(ring_shift(piece, step))

    running = jnp.cumsum(log_decay, axis=1)
    last_sum = running[:, -1:]
    gap = running[:, :, None] - running[:, None, :]
    row_index = lax.broadcasted_iota(jnp.int32, gap.shape, 1)
    col_index = lax.broadcasted_iota(jnp.int32, gap.shape, 2)
    lower_decay = jnp.exp(jnp.where(row_index >= col_index, gap, -1e30))
    to_end = jnp.exp(last_sum - running)
    from_start = jnp.exp(running)
    to_end_wide = jnp.repeat(to_end.T, head_width, axis=1)
    from_start_wide = jnp.repeat(from_start.T, head_width, axis=1)
    skip_wide = jnp.repeat(skip_gain, head_width)[None, :]

    head_x = head_input.astype(f32)
    x_decayed = head_x * to_end_wide
    local_state = exact(x_decayed, write_vector, ((0,), (0,)))
    totals = jnp.broadcast_to(last_sum[:, None, :, None], (heads, BLOCKS // heads, 8, 128))
    packed = jnp.concatenate(
        [local_state.reshape(BLOCKS, 16, 128), totals.reshape(BLOCKS, 8, 128)], axis=1
    )
    packed = swap(packed, CTX)
    weights = block_weights(packed[:, 16, 0])
    entering = chain(weights, packed[:, :16], False)
    start = swap(entering, CTX).reshape(width, 128)
    owns, _ = lax.optimization_barrier((owns, start))
    others = [swap_core(piece) for piece in owns]
    start, weight_rows = lax.optimization_barrier((start, weight_rows))

    scores = mm(read_vector, write_vector, ((1,), (1,)))
    mixed = (lower_decay * scores[None]).astype(bf16)
    x_heads = head_input.reshape(tokens, heads, head_width)
    inner = jnp.einsum("hts,shp->thp", mixed, x_heads, preferred_element_type=f32)
    core_y = inner.reshape(tokens, width) + exact(read_vector, start, ((1,), (1,))) * from_start_wide
    out_y = (core_y + skip_wide * head_x).astype(bf16)

    core_one = jnp.full((1,), core, jnp.int32)
    parts = [
        ring_shift(ring_grad_part(core_one, owns[step], others[step], weight_rows), 4 - step)
        for step in (2, 1, 3)
    ]
    parts.append(ring_grad_part(core_one, owns[0], others[0], weight_rows))
    ring_y = [ring_shift(out_y, step) for step in range(4)]
    parts, _ = lax.optimization_barrier((parts, out_y))
    grad_low = sum(part.astype(f32) for part in parts).astype(bf16)

    partial = weight_grad_part(core_one, owns, others, ring_y)
    weight_grad = lax.psum_scatter(partial, "z", scatter_dimension=0, tiled=True).astype(f32)

    grad = grad_low.astype(f32)
    grad_decayed = grad * from_start_wide
    carried = exact(grad_decayed, read_vector, ((0,), (0,)))
    carried = swap(carried.reshape(BLOCKS, 16, 128), CTX)
    grad_heads = grad_low.reshape(tokens, heads, head_width)
    inner = jnp.einsum("hst,shp->thp", mixed, grad_heads, preferred_element_type=f32)
    inner = inner.reshape(tokens, width)
    entering = chain(weights, carried, True)
    entering, inner = lax.optimization_barrier((entering, inner))
    end = swap(entering, CTX).reshape(width, 128)


    cross_dots = jnp.einsum("thp,shp->hts", grad_heads, x_heads, preferred_element_type=f32)
    pair_weights = jnp.sum(lower_decay * cross_dots, axis=0).astype(bf16)
    read_grad = mm(pair_weights, write_vector, ((1,), (0,))) + mm(
        grad_decayed.astype(bf16), start.astype(bf16), ((1,), (0,))
    )
    write_grad = mm(pair_weights, read_vector, ((0,), (0,))) + mm(
        x_decayed.astype(bf16), end.astype(bf16), ((1,), (0,))
    )

    skip_part = jnp.sum((grad * head_x).reshape(tokens, heads, head_width), axis=(0, 2))
    square_part = jnp.sum((weight_grad * weight_grad).reshape(-1, heads, head_width), axis=(0, 2))
    small = jnp.concatenate([skip_part, square_part, jnp.zeros((112,), f32)])

    both = jnp.concatenate([write_grad, read_grad], axis=0)
    keep = lax.dynamic_slice_in_dim(both, core * tokens, tokens, axis=0)
    give = lax.dynamic_slice_in_dim(both, (1 - core) * tokens, tokens, axis=0)
    mine = (keep + swap_core(give)).astype(bf16)
    mine, end, small = lax.optimization_barrier((mine, end, small))
    small = spread(jnp.broadcast_to(small[None], (8, 128)), CTX, BLOCKS)
    small = jnp.sum(small, axis=0)[0]
    column = lax.axis_index("y")
    terms = [mine] + [
        lax.ppermute(mine, "y", [(i, (i + step) % 4) for i in range(4)]) for step in range(1, 4)
    ]
    terms, small = lax.optimization_barrier((terms, small))
    keep = 0.0
    for y in range(4):
        keep = keep + lax.select_n(lax.rem(column + 4 - y, 4), *terms).astype(f32)
    give = swap_core(keep)
    write_sum = jnp.where(core == 0, keep, give)
    read_sum = jnp.where(core == 0, give, keep)

    core_grad = inner + exact(write_vector, end, ((1,), (1,))) * to_end_wide
    input_grad = (core_grad + skip_wide * grad).astype(bf16)

    terms = (grad * core_y - head_x * core_grad).reshape(tokens, heads, head_width)
    decay_part = jnp.sum(terms, axis=2).T
    local_tail = jnp.flip(jnp.cumsum(jnp.flip(decay_part, 1), axis=1), 1)
    end_state = start.reshape(heads, -1) * jnp.exp(last_sum) + local_state.reshape(
        heads, -1
    )
    above = jnp.sum(end_state * end.reshape(heads, -1), axis=1)
    decay_grad = local_tail + above[:, None]

    skip_total, square_total = small[:heads], small[heads : 2 * heads]
    mean_square = square_total / float(WIDTH * head_width)
    new_second = beta_two * squared_average + (1.0 - beta_two) * mean_square
    new_first = beta_one * first_moment + (1.0 - beta_one) * weight_grad
    scale = jnp.repeat(jnp.sqrt(new_second / bias_two) + adam_eps, head_width)
    new_master = out_master - learn_rate * (
        new_first / bias_one / scale[None, :] + decoupled_decay * out_master
    )
    return (
        input_grad,
        write_sum,
        read_sum,
        decay_grad,
        skip_total,
        new_master,
        new_first,
        new_second,
    )


def solution(mesh):
    fine = Mesh(mesh.devices.reshape(4, 8, 4, 2), ("x", "z", "y", "core"))
    in_specs = (
        P(CTX, TP),
        P(CTX, None),
        P(CTX, None),
        P(TP, CTX),
        P(TP),
        P(CTX, None),
        P(CTX, TP),
        P(CTX, TP),
        P(TP),
    )
    out_specs = (
        P(CTX, TP),
        P(CTX, None),
        P(CTX, None),
        P(TP, CTX),
        P(TP),
        P(CTX, TP),
        P(CTX, TP),
        P(TP),
    )
    return jax.shard_map(shards, mesh=fine, in_specs=in_specs, out_specs=out_specs, check_vma=False)
```

```python
import jax
import jax.numpy as jnp
from jax import lax
from jax.experimental import pallas as pl
from jax.experimental.pallas import tpu as pltpu
from jax.sharding import Mesh, PartitionSpec as P

WIDTH = 4096
beta_one = 0.9
beta_two = 0.95
learn_rate = 0.004
decoupled_decay = 0.1
adam_eps = 1e-08
bias_one = 0.9999734386011124
bias_two = 0.994079470779666

f32 = jnp.float32
bf16 = jnp.bfloat16
CTX = ("x", "z")
TP = ("y", "core")
BLOCKS = 32


def mm(a, b, dims):
    return lax.dot_general(a, b, (dims, ((), ())), preferred_element_type=f32)


def block_weights(logs):
    i = lax.broadcasted_iota(jnp.int32, (BLOCKS, BLOCKS, BLOCKS), 0)
    j = lax.broadcasted_iota(jnp.int32, (BLOCKS, BLOCKS, BLOCKS), 1)
    r = lax.broadcasted_iota(jnp.int32, (BLOCKS, BLOCKS, BLOCKS), 2)
    between = jnp.sum(jnp.where((r > j) & (r < i), logs[None, None, :], 0.0), axis=2)
    rows = lax.broadcasted_iota(jnp.int32, (BLOCKS, BLOCKS), 0)
    cols = lax.broadcasted_iota(jnp.int32, (BLOCKS, BLOCKS), 1)
    return jnp.where(rows > cols, jnp.exp(between), 0.0)


def exact(a, b, dims):
    return lax.dot_general(
        a.astype(f32),
        b.astype(f32),
        (dims, ((), ())),
        precision=lax.Precision.HIGHEST,
        preferred_element_type=f32,
    )


def swap(value, axes):
    return lax.all_to_all(value, axes, 0, 0, tiled=True)


def swap_core(value):
    return lax.ppermute(value, "core", [(0, 1), (1, 0)])


def ring_shift(value, step):
    return lax.ppermute(value, "x", [(i, (i + step) % 4) for i in range(4)]) if step else value


def spread(value, axis, count):
    return swap(jnp.broadcast_to(value[None], (count,) + value.shape), axis)


TILE = 256
ANYWHERE = pl.BlockSpec(memory_space=pl.ANY)
IN_SMEM = pl.BlockSpec(memory_space=pltpu.SMEM)
IN_VMEM = pl.BlockSpec(memory_space=pltpu.VMEM)


def tile_of(j):
    return pl.ds(pl.multiple_of(j * TILE, TILE), TILE)


def fetch(refs, buffers, sems):
    copies = [
        pltpu.make_async_copy(ref, buffer, sems.at[i])
        for i, (ref, buffer) in enumerate(zip(refs, buffers))
    ]
    for copy in copies:
        copy.start()
    return copies


def like(arrays):
    return [pltpu.VMEM(a.shape, a.dtype) for a in arrays] + [pltpu.SemaphoreType.DMA((len(arrays),))]


def ring_grad_kernel(core_ref, own_in, other_in, weight_in, out_ref, own_ref, other_ref, weight_ref, sems):
    copies = fetch((weight_in, own_in, other_in), (weight_ref, own_ref, other_ref), sems)
    half = own_ref.shape[0]
    core = core_ref[0]
    copies[0].wait()
    for copy, ref, at in zip(copies[1:], (own_ref, other_ref), (core, 1 - core)):
        copy.wait()
        out_ref[pl.ds(pl.multiple_of(at * half, half), half), :] = jnp.dot(
            ref[...], weight_ref[...], preferred_element_type=f32
        ).astype(bf16)


def ring_grad_part(core, own, other, weight_rows):
    half, quarter = own.shape
    width = weight_rows.shape[1]
    return pl.pallas_call(
        ring_grad_kernel,
        out_shape=jax.ShapeDtypeStruct((2 * half, width), bf16),
        in_specs=[IN_SMEM] + [ANYWHERE] * 3,
        out_specs=IN_VMEM,
        scratch_shapes=like((own, other, weight_rows)),
        cost_estimate=pl.CostEstimate(
            flops=4 * half * quarter * width, bytes_accessed=3 << 20, transcendentals=0
        ),
        compiler_params=pltpu.CompilerParams(vmem_limit_bytes=16 << 20),
        name="ring_grad",
    )(core, own, other, weight_rows)


def weight_grad_kernel(core_ref, *refs):
    out_ref, sems = refs[12], refs[25]
    for copy in fetch(refs[:12], refs[13:25], sems):
        copy.wait()
    owns, others, ys = refs[13:17], refs[17:21], refs[21:25]
    half = owns[0].shape[0]
    core = core_ref[0]

    @pl.loop(0, out_ref.shape[0] // TILE)
    def _(j):
        total = None
        for own, other, y in zip(owns, others, ys):
            for ref, at in ((own, core), (other, 1 - core)):
                part = lax.dot_general(
                    ref[:, tile_of(j)],
                    y[pl.ds(pl.multiple_of(at * half, half), half), :],
                    (((0,), (0,)), ((), ())),
                    preferred_element_type=f32,
                )
                total = part if total is None else total + part
        out_ref[tile_of(j), :] = total.astype(bf16)


def weight_grad_part(core, owns, others, ys):
    half, quarter = owns[0].shape
    width = ys[0].shape[1]
    return pl.pallas_call(
        weight_grad_kernel,
        out_shape=jax.ShapeDtypeStruct((quarter, width), bf16),
        in_specs=[IN_SMEM] + [ANYWHERE] * 12,
        out_specs=IN_VMEM,
        scratch_shapes=like((*owns, *others, *ys)),
        cost_estimate=pl.CostEstimate(
            flops=16 * half * quarter * width, bytes_accessed=8 << 20, transcendentals=0
        ),
        compiler_params=pltpu.CompilerParams(vmem_limit_bytes=24 << 20),
        name="weight_grad",
    )(core, *owns, *others, *ys)


def chain(weights, parts, reverse):
    dims = ((0,), (0,)) if reverse else ((1,), (0,))
    out = exact(weights, parts.reshape(BLOCKS, 16 * 128), dims)
    return out.reshape(BLOCKS, 16, 128)


def shards(
    head_input,
    write_vector,
    read_vector,
    log_decay,
    skip_gain,
    out_grad,
    out_master,
    first_moment,
    squared_average,
):
    tokens, width = head_input.shape
    heads = log_decay.shape[0]
    head_width = width // heads

    core = lax.axis_index("core")
    ring = lax.axis_index("x")
    half = tokens // 2
    quarter = WIDTH // 4

    weight_rows = lax.all_gather(out_master.astype(bf16), "z", axis=0, tiled=True)
    owns = []
    for step in range(4):
        to = lax.rem(ring + step, 4)
        piece = lax.dynamic_slice(out_grad, (core * half, to * quarter), (half, quarter))
        owns.append(ring_shift(piece, step))

    running = jnp.cumsum(log_decay, axis=1)
    last_sum = running[:, -1:]
    gap = running[:, :, None] - running[:, None, :]
    row_index = lax.broadcasted_iota(jnp.int32, gap.shape, 1)
    col_index = lax.broadcasted_iota(jnp.int32, gap.shape, 2)
    lower_decay = jnp.exp(jnp.where(row_index >= col_index, gap, -1e30))
    to_end = jnp.exp(last_sum - running)
    from_start = jnp.exp(running)
    to_end_wide = jnp.repeat(to_end.T, head_width, axis=1)
    from_start_wide = jnp.repeat(from_start.T, head_width, axis=1)
    skip_wide = jnp.repeat(skip_gain, head_width)[None, :]

    head_x = head_input.astype(f32)
    x_decayed = head_x * to_end_wide
    local_state = exact(x_decayed, write_vector, ((0,), (0,)))
    totals = jnp.broadcast_to(last_sum[:, None, :, None], (heads, BLOCKS // heads, 8, 128))
    packed = jnp.concatenate(
        [local_state.reshape(BLOCKS, 16, 128), totals.reshape(BLOCKS, 8, 128)], axis=1
    )
    packed = swap(packed, CTX)
    weights = block_weights(packed[:, 16, 0])
    entering = chain(weights, packed[:, :16], False)
    start = swap(entering, CTX).reshape(width, 128)

    scores = mm(read_vector, write_vector, ((1,), (1,)))
    mixed = (lower_decay * scores[None]).astype(bf16)
    x_heads = head_input.reshape(tokens, heads, head_width)
    inner = jnp.einsum("hts,shp->thp", mixed, x_heads, preferred_element_type=f32)
    inner = inner.reshape(tokens, width)
    owns, inner, from_start_wide = lax.optimization_barrier((owns, inner, from_start_wide))
    others = [swap_core(piece) for piece in owns]
    start, weight_rows = lax.optimization_barrier((start, weight_rows))
    core_y = inner + exact(read_vector, start, ((1,), (1,))) * from_start_wide
    out_y = (core_y + skip_wide * head_x).astype(bf16)

    core_one = jnp.full((1,), core, jnp.int32)
    parts = [
        ring_shift(ring_grad_part(core_one, owns[step], others[step], weight_rows), 4 - step)
        for step in (2, 1, 3)
    ]
    parts.append(ring_grad_part(core_one, owns[0], others[0], weight_rows))
    ring_y = [ring_shift(out_y, step) for step in range(4)]
    parts, _ = lax.optimization_barrier((parts, out_y))
    grad_low = sum(part.astype(f32) for part in parts).astype(bf16)

    partial = weight_grad_part(core_one, owns, others, ring_y)
    weight_grad = lax.psum_scatter(partial, "z", scatter_dimension=0, tiled=True).astype(f32)

    grad = grad_low.astype(f32)
    grad_decayed = grad * from_start_wide
    carried = exact(grad_decayed, read_vector, ((0,), (0,)))
    carried = swap(carried.reshape(BLOCKS, 16, 128), CTX)
    grad_heads = grad_low.reshape(tokens, heads, head_width)
    inner = jnp.einsum("hst,shp->thp", mixed, grad_heads, preferred_element_type=f32)
    inner = inner.reshape(tokens, width)
    entering = chain(weights, carried, True)
    entering, inner = lax.optimization_barrier((entering, inner))
    end = swap(entering, CTX).reshape(width, 128)


    cross_dots = jnp.einsum("thp,shp->hts", grad_heads, x_heads, preferred_element_type=f32)
    pair_weights = jnp.sum(lower_decay * cross_dots, axis=0).astype(bf16)
    read_grad = mm(pair_weights, write_vector, ((1,), (0,))) + mm(
        grad_decayed.astype(bf16), start.astype(bf16), ((1,), (0,))
    )
    write_grad = mm(pair_weights, read_vector, ((0,), (0,))) + mm(
        x_decayed.astype(bf16), end.astype(bf16), ((1,), (0,))
    )

    skip_part = jnp.sum((grad * head_x).reshape(tokens, heads, head_width), axis=(0, 2))
    square_part = jnp.sum((weight_grad * weight_grad).reshape(-1, heads, head_width), axis=(0, 2))
    small = jnp.concatenate([skip_part, square_part, jnp.zeros((112,), f32)])

    both = jnp.concatenate([write_grad, read_grad], axis=0)
    keep = lax.dynamic_slice_in_dim(both, core * tokens, tokens, axis=0)
    give = lax.dynamic_slice_in_dim(both, (1 - core) * tokens, tokens, axis=0)
    mine = (keep + swap_core(give)).astype(bf16)
    mine, end, small = lax.optimization_barrier((mine, end, small))
    small = spread(jnp.broadcast_to(small[None], (8, 128)), CTX, BLOCKS)
    small = jnp.sum(small, axis=0)[0]
    column = lax.axis_index("y")
    terms = [mine] + [
        lax.ppermute(mine, "y", [(i, (i + step) % 4) for i in range(4)]) for step in range(1, 4)
    ]
    terms, small = lax.optimization_barrier((terms, small))
    keep = 0.0
    for y in range(4):
        keep = keep + lax.select_n(lax.rem(column + 4 - y, 4), *terms).astype(f32)
    give = swap_core(keep)
    write_sum = jnp.where(core == 0, keep, give)
    read_sum = jnp.where(core == 0, give, keep)

    core_grad = inner + exact(write_vector, end, ((1,), (1,))) * to_end_wide
    input_grad = (core_grad + skip_wide * grad).astype(bf16)

    terms = (grad * core_y - head_x * core_grad).reshape(tokens, heads, head_width)
    decay_part = jnp.sum(terms, axis=2).T
    local_tail = jnp.flip(jnp.cumsum(jnp.flip(decay_part, 1), axis=1), 1)
    end_state = start.reshape(heads, -1) * jnp.exp(last_sum) + local_state.reshape(
        heads, -1
    )
    above = jnp.sum(end_state * end.reshape(heads, -1), axis=1)
    decay_grad = local_tail + above[:, None]

    skip_total, square_total = small[:heads], small[heads : 2 * heads]
    mean_square = square_total / float(WIDTH * head_width)
    new_second = beta_two * squared_average + (1.0 - beta_two) * mean_square
    new_first = beta_one * first_moment + (1.0 - beta_one) * weight_grad
    scale = jnp.repeat(jnp.sqrt(new_second / bias_two) + adam_eps, head_width)
    new_master = out_master - learn_rate * (
        new_first / bias_one / scale[None, :] + decoupled_decay * out_master
    )
    return (
        input_grad,
        write_sum,
        read_sum,
        decay_grad,
        skip_total,
        new_master,
        new_first,
        new_second,
    )


def solution(mesh):
    fine = Mesh(mesh.devices.reshape(4, 8, 4, 2), ("x", "z", "y", "core"))
    in_specs = (
        P(CTX, TP),
        P(CTX, None),
        P(CTX, None),
        P(TP, CTX),
        P(TP),
        P(CTX, None),
        P(CTX, TP),
        P(CTX, TP),
        P(TP),
    )
    out_specs = (
        P(CTX, TP),
        P(CTX, None),
        P(CTX, None),
        P(TP, CTX),
        P(TP),
        P(CTX, TP),
        P(CTX, TP),
        P(TP),
    )
    return jax.shard_map(shards, mesh=fine, in_specs=in_specs, out_specs=out_specs, check_vma=False)
```
